512 devices in a mesh: fsdp: 32 (over y, z_hi, core), ctx: 16 (over z_lo, x).
Axes of the slice: x: 4, y: 8, z: 8 (z_hi: 2, z_lo: 4; z = z_hi * 4 + z_lo), core: 2. Of those that a mesh axis runs over, the one named last changes fastest.
Arguments:
- byte_ids: int32 [32, 16384], P('fsdp', 'ctx'), may hold values from 0 to 255
- byte_table: bfloat16 [256, 768], replicated, may hold values from -6 to 6
- w_conv: bfloat16 [3072, 1024], P('fsdp'), may hold values from -0.109375 to 0.109375
- w_qkv: bfloat16 [1024, 1536], P('fsdp'), may hold values from -4 to 4
- w_out: bfloat16 [1024, 1024], P('fsdp'), may hold values from -0.1875 to 0.1875
- norm_gain: bfloat16 [1024], replicated, may hold values from 0.5 to 1.5
- teacher: bfloat16 [32, 4096, 1024], P('fsdp', 'ctx'), may hold values from -6 to 6
- align: int32 [32, 4096], P('fsdp', 'ctx'), may hold values from 0 to 4095, as said below
Outputs:
- hidden_out: bfloat16 [32, 4096, 1024], P('fsdp', 'ctx')
- token_loss: float32 [32, 4096], P('fsdp', 'ctx')
The draws below stay inside these ranges and needn't reach their ends.
Inputs may be any that keep to these rules, and one draw needn't show every extreme that they name: Teacher token j of a sequence points at a latent of its own aligned block of 256 rows (align // 256 == j // 256); the first and the last token of each block point at that block's first and last latent.
All inputs are finite; a program needn't handle non-finite values.
Results may differ from the reference program's by a relative error of at most 0.039.
Values may be sent and summed in bfloat16 or wider, within the bound.
A program may use at most 64 MiB of HBM per device.

```python
import math
import jax
import jax.numpy as jnp
import numpy as np
from jax import lax

D = 1024
E = 768
KW = 4
BYTE_VOCAB = 256
HQ = 16
HK = 4
HD = 64
LAT_DEV = 256
GROUP = 4
QKV = 1536
LATENTS = 4096
BYTES = 16384
SEQS = 32


def draw_w_qkv(key, part):
    key = jax.random.fold_in(key, 11)
    base = jax.random.truncated_normal(key, -6.0, 6.0, (D, QKV), jnp.float32) / math.sqrt(D)
    column = jnp.arange(QKV, dtype=jnp.int32)
    lift = jnp.where(column < HQ * HD + HK * HD, 2.0, 1.0).astype(jnp.float32)
    base = base * lift[None, :]
    return jnp.clip(base, -4.0, 4.0).astype(jnp.bfloat16)


def draw_align(key, part):
    key = jax.random.fold_in(key, 5)
    row_index = jnp.arange(LATENTS, dtype=jnp.int32)
    block_first = row_index // LAT_DEV * LAT_DEV
    in_block = row_index % LAT_DEV
    offsets = jax.random.randint(key, (SEQS, LATENTS), 0, LAT_DEV, dtype=jnp.int32)
    offsets = jnp.where(in_block[None, :] == 0, 0, offsets)
    offsets = jnp.where(in_block[None, :] == LAT_DEV - 1, LAT_DEV - 1, offsets)
    return (block_first[None, :] + offsets).astype(jnp.int32)


def with_ends(drawn, stream_key, least, largest):
    longest = drawn.shape.index(max(drawn.shape))
    spots = []
    for shift in (0, 1):
        where = [jax.random.randint(jax.random.fold_in(stream_key, axis), (), 0, length) for axis, length in enumerate(drawn.shape)]
        where[longest] = (where[longest] + shift) % drawn.shape[longest]
        spots.append(tuple(where))
    return drawn.at[spots[0]].set(least).at[spots[1]].set(largest)


def block_scale(own_key, dims, split, smallest, largest):
    def one(dim, parts):
        heights = jax.random.uniform(jax.random.fold_in(jax.random.fold_in(own_key, 6), dim), (parts,), jnp.float32, smallest / len(split), largest / len(split))
        return jnp.repeat(jnp.exp(heights), dims[dim] // parts).reshape((-1,) + (1,) * (len(dims) - dim - 1))

    loudness = one(*split[0])
    for cut in split[1:]:
        loudness = loudness * one(*cut)
    return loudness


def cumulative_ranks(number_of, lean):
    portions = [(1 << 20) // math.isqrt(grade ** lean) + 1 for grade in range(1, number_of + 1)]
    spread = 1 + sum(portions) // (1 << 30)
    return np.cumsum(np.array([max(1, weight // spread) for weight in portions]))


def ranked_ids(key, extent, amount, skew):
    table = cumulative_ranks(amount, skew)
    pick = jax.random.randint(jax.random.fold_in(key, 1), extent, 0, int(table[amount - 1]))
    standing = jnp.searchsorted(jnp.asarray(table, jnp.int32), pick, side="right")
    return jax.random.permutation(jax.random.fold_in(key, 2), amount)[standing].astype(jnp.int32)


def gaussian(rng, extent, scale, reach, shards=(), kind=jnp.bfloat16):
    result = jax.random.normal(rng, extent, jnp.float32) * scale
    if len(shards) > 0:
        result = block_scale(rng, extent, shards, -0.22, 0.18) * result
    return jnp.clip(result, min=-reach, max=reach).astype(kind)


def setup_inputs(seed: int = 0) -> dict:
    arg_keys = jax.random.split(jax.random.key(seed), 9)
    byte_ids = with_ends(ranked_ids(arg_keys[0], (SEQS, BYTES), BYTE_VOCAB, 2), jax.random.fold_in(arg_keys[0], 3), 0, BYTE_VOCAB - 1).astype(jnp.int32)
    byte_table = gaussian(arg_keys[1], (BYTE_VOCAB, E), 1.0, 6.0)
    w_conv = gaussian(arg_keys[2], (KW * E, D), (KW * E) ** -0.5, 0.109375, ((0, 32),))
    w_qkv = draw_w_qkv(jax.random.fold_in(arg_keys[8], 71), 0)
    w_out = gaussian(arg_keys[4], (HQ * HD, D), (HQ * HD) ** -0.5, 0.1875, ((0, 32),))
    norm_gain = jnp.clip(jax.random.uniform(arg_keys[5], (D,), jnp.float32, 0.5, 1.5), 0.5, 1.5).astype(jnp.bfloat16)
    teacher = gaussian(arg_keys[6], (SEQS, LATENTS, D), 1.0, 6.0, ((0, 32), (1, 16)))
    align = draw_align(jax.random.fold_in(arg_keys[8], 71), 0)
    return {"byte_ids": byte_ids, "byte_table": byte_table, "w_conv": w_conv, "w_qkv": w_qkv, "w_out": w_out, "norm_gain": norm_gain, "teacher": teacher, "align": align}


theta_base = 500000.0
norm_eps = 1e-05

def rotate(values, positions):
    half_dim = values.shape[-1] // 2
    frequency = theta_base ** (-jnp.arange(half_dim, dtype=jnp.float32) * 2.0 / values.shape[-1])
    angles = positions.astype(jnp.float32)[:, None] * frequency[None, :]
    angles = jnp.concatenate([angles, angles], axis=-1)[:, None, :]
    turned = jnp.concatenate([-values[..., half_dim:], values[..., :half_dim]], axis=-1)
    return values * jnp.cos(angles) + turned * jnp.sin(angles)

def reference(byte_ids, byte_table, w_conv, w_qkv, w_out, norm_gain, teacher, align):
    score_scale = 1.0 / math.sqrt(HD)
    query_width = HQ * HD
    key_width = HK * HD

    def one_sequence(inputs):
        sequence_ids, teach_rows, aligned = inputs
        embedded = byte_table[sequence_ids]
        stacked = embedded.reshape(LATENTS, KW * E)
        latent = jnp.dot(stacked, w_conv, preferred_element_type=jnp.float32).astype(jnp.bfloat16)
        latent_wide = latent.astype(jnp.float32)
        scale_rows = lax.rsqrt(lax.optimization_barrier(jnp.mean(latent_wide * latent_wide, axis=1, keepdims=True)) + norm_eps)
        normed = (latent_wide * scale_rows * norm_gain.astype(jnp.float32)[None, :]).astype(jnp.bfloat16)
        projected = jnp.dot(normed, w_qkv, preferred_element_type=jnp.float32)
        positions = jnp.arange(LATENTS, dtype=jnp.int32)
        queries = rotate(projected[:, :query_width].reshape(LATENTS, HQ, HD), positions).astype(jnp.bfloat16)
        key_rows = rotate(projected[:, query_width:query_width + key_width].reshape(LATENTS, HK, HD), positions).astype(jnp.bfloat16)
        value_rows = projected[:, query_width + key_width:].reshape(LATENTS, HK, HD).astype(jnp.bfloat16)
        allowed = positions[None, :] <= positions[:, None]

        def head_out(head):
            query_head = lax.dynamic_index_in_dim(queries, head, axis=1, keepdims=False)
            group_index = head // GROUP
            key_head = lax.dynamic_index_in_dim(key_rows, group_index, axis=1, keepdims=False)
            value_head = lax.dynamic_index_in_dim(value_rows, group_index, axis=1, keepdims=False)
            scores = jnp.dot(query_head, key_head.T, preferred_element_type=jnp.float32) * score_scale
            scores = jnp.where(allowed, scores, -jnp.inf)
            row_top = lax.optimization_barrier(jnp.max(scores, axis=1, keepdims=True))
            probs = jnp.exp(scores - row_top)
            row_mass = lax.optimization_barrier(jnp.sum(probs, axis=1, keepdims=True))
            summed = jnp.dot(probs.astype(jnp.bfloat16), value_head, preferred_element_type=jnp.float32)
            return summed / row_mass
        heads = lax.map(head_out, jnp.arange(HQ, dtype=jnp.int32))
        attended = jnp.transpose(heads, (1, 0, 2)).reshape(LATENTS, HQ * HD).astype(jnp.bfloat16)
        branch = jnp.dot(attended, w_out, preferred_element_type=jnp.float32)
        hidden_out = (latent_wide + branch).astype(jnp.bfloat16)
        picked = jnp.take(hidden_out, aligned, axis=0)
        difference = picked.astype(jnp.float32) - teach_rows.astype(jnp.float32)
        token_loss = lax.optimization_barrier(jnp.mean(difference * difference, axis=1))
        return (hidden_out, token_loss)
    hidden_all, loss_all = lax.map(one_sequence, (byte_ids, teacher, align))
    return (hidden_all, loss_all)
```

```python
import math

import jax
import jax.numpy as jnp
import numpy as np
from jax import lax
from jax.experimental import pallas as pl
from jax.experimental.pallas import tpu as pltpu
from jax.sharding import PartitionSpec as P

KW = 4
HQ = 16
HK = 4
HD = 64
D = 1024
BLK = 256
NCTX = 16
theta_base = 500000.0
norm_eps = 1e-05
masked_score = -1e30
MESH = pl.DeviceIdType.MESH
F32 = jnp.float32
BF16 = jnp.bfloat16


def rope_tables(length):
    half = HD // 2
    frequency = theta_base ** (-np.arange(half, dtype=np.float64) * 2.0 / HD)
    angles = frequency[:, None] * np.arange(length, dtype=np.float64)[None, :]
    return np.cos(angles).astype(np.float32), np.sin(angles).astype(np.float32)


def rc(src, dst, send, recv, dev):
    return pltpu.make_async_remote_copy(
        src_ref=src, dst_ref=dst, send_sem=send, recv_sem=recv, device_id=dev, device_id_type=MESH
    )


def tn(a, b):
    return lax.dot_general(a, b, (((0,), (0,)), ((), ())), preferred_element_type=F32)


def kernel(
    ids_ref, bt_ref, wc_ref, wq_ref, wo_ref, cos_ref, sin_ref, teach_ref, align_ref,
    hid_ref, loss_ref,
    ids_all, scale_all, wc_all, tt, wg, wo, ut, k_scr, vt_scr, qt_scr, lat_scr, att_out, att_in,
    ids_s, ids_r, sc_s, sc_r, wc_s, wc_r, ty_s, ty_r, t3_s, t3_r, t4_s, t4_r, t5_s, t5_r,
    wg_s, wg_r, wgx_s, wgx_r, wo_s, wo_r, wo2_s, wo2_r, wo3_s, wo3_r, at_s, at_r,
):
    f = lax.axis_index("fsdp")
    c = lax.axis_index("ctx")
    g, core = f // 2, f % 2
    y, zh = f // 4, (f // 2) % 2
    zl, x = c // 4, c % 4
    tap = f // 8
    sib = (f // 2) * 2 + 1 - core
    zfull = zh * 4 + zl

    def same_core(i):
        return (((g + i) % 16) * 2 + core, c)

    def ctx_peer(i):
        return (f, (c + i) % NCTX)

    def mate(i):
        return (tap * 8 + (f % 8 + i) % 8, c)

    def z_dev(step):
        z2 = (zfull + step + 8) % 8
        return (y * 4 + (z2 // 4) * 2 + core, (z2 % 4) * 4 + x)

    def x_dev(step):
        return (f, zl * 4 + (x + step + 4) % 4)

    barrier = pltpu.get_barrier_semaphore()

    def sig(dev):
        pl.semaphore_signal(barrier, inc=1, device_id=dev, device_id_type=MESH)

    def loop(lo, hi, fn):
        def step(i, carry):
            fn(i)
            return carry

        lax.fori_loop(lo, hi, step, 0)

    loop(1, 16, lambda i: sig(same_core(i)))
    loop(1, 16, lambda i: sig(ctx_peer(i)))
    loop(1, 8, lambda i: sig(mate(i)))
    sig((sib, c))
    sig(z_dev(1))
    sig(z_dev(-1))
    sig(z_dev(-2))
    pl.semaphore_wait(barrier, 15 + 15 + 7 + 1 + 3)

    def wc_copy(i, slot):
        return rc(wc_ref, wc_all.at[slot], wc_s.at[i], wc_r.at[i], mate(i))

    loop(1, 8, lambda i: wc_copy(i, f % 8).start())
    wc_all[f % 8] = wc_ref[...]

    def ids_copy(i, slot):
        return rc(ids_ref, ids_all.at[slot], ids_s.at[i], ids_r.at[i], ctx_peer(i))

    loop(1, 16, lambda i: ids_copy(i, c).start())
    ids_all[c] = ids_ref[...]

    def wg_copy(i, slot):
        return rc(wq_ref, wg.at[slot, core], wg_s.at[i], wg_r.at[i], same_core(i))

    loop(1, 16, lambda i: wg_copy(i, g).start())
    wg[g, core] = wq_ref[...]

    btt = bt_ref[...].T
    bta = jnp.concatenate([btt[m * 96 : m * 96 + 48] for m in range(8)], axis=0)
    btb = jnp.concatenate([btt[m * 96 + 48 : m * 96 + 96] for m in range(8)], axis=0)

    loop(1, 8, lambda i: wc_copy(i, (f % 8 - i + 8) % 8).wait_recv())
    wc_val = wc_all[...].reshape(384, 128)
    piece = tn(wc_val, bta)[:64] + tn(wc_val, btb)[64:]
    half = pl.ds(pl.multiple_of(core * 512, 512), 512)

    def y_dev(step):
        return (((y + 2 * step) % 8) * 4 + zh * 2 + core, c)

    def y_copy(step, from_tap):
        ref = tt.at[zl, x, :, pl.ds(pl.multiple_of(from_tap * 256, 256), 256)]
        return rc(ref, ref, ty_s.at[step], ty_r.at[step], y_dev(step))

    @pl.when(tap // 2 == core)
    def _():
        tt[zl, x, :, pl.ds(pl.multiple_of(tap * 256, 256), 256)] = piece.astype(BF16)
        for step in (1, 2, 3):
            y_copy(step, tap).start()

    for step in (1, 2, 3):
        src_tap = (tap - step + 4) % 4

        @pl.when(src_tap // 2 == core)
        def _():
            y_copy(step, src_tap).wait_recv()

    own = tt.at[zl, x, :, half]

    def first_copy(n, dev, ref):
        return rc(ref, ref, t3_s.at[n], t3_r.at[n], dev)

    steps = (1, -1, 2)

    @pl.when(core == 0)
    def _():
        for n, s in enumerate(steps):
            first_copy(n, z_dev(s), own).start()
        for n, s in enumerate(steps):
            first_copy(n, z_dev(s), tt.at[(zl - s + 4) % 4, x, :, half]).wait_recv()
        for n, s in enumerate(steps):
            ref = tt.at[:, x, :, half]
            rc(ref, ref, t4_s.at[n], t4_r.at[n], x_dev(s)).start()

    @pl.when(core == 1)
    def _():
        for n, s in enumerate(steps):
            first_copy(n, x_dev(s), own).start()
        for n, s in enumerate(steps):
            first_copy(n, x_dev(s), tt.at[zl, (x - s + 4) % 4, :, half]).wait_recv()
        for n, s in enumerate(steps):
            ref = tt.at[zl, :, :, half]
            rc(ref, ref, t4_s.at[n], t4_r.at[n], z_dev(s)).start()

    loop(1, 16, lambda i: wg_copy(i, (g - i + 16) % 16).wait_recv())
    rc(wg.at[:, core], wg.at[:, core], wgx_s.at[0], wgx_r.at[0], (sib, c)).start()

    def wo_copy(i, slot):
        return rc(
            wo_ref.at[:, pl.ds(pl.multiple_of(x * 256, 256), 256)],
            wo.at[x, slot, core], wo_s.at[i], wo_r.at[i], same_core(i),
        )

    loop(1, 16, lambda i: wo_copy(i, g).start())
    wo[x, g, core] = wo_ref[:, pl.ds(pl.multiple_of(x * 256, 256), 256)]

    @pl.when(core == 0)
    def _():
        ref = tt.at[:, x, :, half]
        rc(ref, ref, t5_s.at[0], t5_r.at[0], (sib, c)).start()
        for n, s in enumerate(steps):
            ref = tt.at[:, (x - s + 4) % 4, :, half]
            rc(ref, ref, t4_s.at[n], t4_r.at[n], x_dev(s)).wait_recv()
            rc(ref, ref, t5_s.at[n + 1], t5_r.at[n + 1], (sib, c)).start()
        other = pl.ds(512, 512)
        for n, s in enumerate((0,) + steps):
            ref = tt.at[(zl - s + 4) % 4, :, :, other]
            rc(ref, ref, t5_s.at[n], t5_r.at[n], (sib, c)).wait_recv()

    @pl.when(core == 1)
    def _():
        ref = tt.at[zl, :, :, half]
        rc(ref, ref, t5_s.at[0], t5_r.at[0], (sib, c)).start()
        for n, s in enumerate(steps):
            ref = tt.at[(zl - s + 4) % 4, :, :, half]
            rc(ref, ref, t4_s.at[n], t4_r.at[n], z_dev(s)).wait_recv()
            rc(ref, ref, t5_s.at[n + 1], t5_r.at[n + 1], (sib, c)).start()
        other = pl.ds(0, 512)
        for n, s in enumerate((0,) + steps):
            ref = tt.at[:, (x - s + 4) % 4, :, other]
            rc(ref, ref, t5_s.at[n], t5_r.at[n], (sib, c)).wait_recv()

    def one_hot(b):
        rows = lax.broadcasted_iota(jnp.int32, (256, BLK), 0)
        block = ids_all[b]
        return jnp.concatenate(
            [(block[k : k + 1, :] == rows).astype(BF16) for k in range(KW)], axis=0
        )

    tall = tt[...].reshape(D, D)
    latent = jnp.dot(tall, one_hot(c), preferred_element_type=F32).astype(BF16)
    wide = latent.astype(F32)
    scale = lax.rsqrt(jnp.sum(wide * wide, axis=0, keepdims=True) * (1.0 / D) + norm_eps)
    scale_all[c] = scale

    def sc_copy(i, slot):
        ref = scale_all.at[slot]
        return rc(ref, ref, sc_s.at[i], sc_r.at[i], ctx_peer(i))

    loop(1, 16, lambda i: sc_copy(i, c).start())
    lat_scr[...] = latent.T

    ref = wg.at[:, 1 - core]
    rc(ref, ref, wgx_s.at[0], wgx_r.at[0], (sib, c)).wait_recv()
    ut[...] = tn(wg[...].reshape(D, 384), tall).astype(BF16)

    loop(1, 16, lambda i: wo_copy(i, (g - i + 16) % 16).wait_recv())

    def wo2_copy(n, s, slot):
        ref = wo.at[slot, :, core]
        return rc(ref, ref, wo2_s.at[n], wo2_r.at[n], x_dev(s))

    for n, s in enumerate(steps):
        wo2_copy(n, s, x).start()

    loop(1, 16, lambda i: ids_copy(i, (c - i + NCTX) % NCTX).wait_recv())
    loop(1, 16, lambda i: sc_copy(i, (c - i + NCTX) % NCTX).wait_recv())

    def turn(v, b, scale_row):
        cols = pl.ds(pl.multiple_of(b * BLK, BLK), BLK)
        cos, sin = cos_ref[:, cols] * scale_row, sin_ref[:, cols] * scale_row
        lo, hi = v[:32], v[32:]
        return jnp.concatenate([lo * cos - hi * sin, hi * cos + lo * sin], axis=0)

    def make_kv(b, carry):
        cols = pl.ds(pl.multiple_of(b * BLK, BLK), BLK)
        kv = jnp.dot(ut[256:384, :], one_hot(b), preferred_element_type=F32)
        k_scr[pl.ds(pl.multiple_of(b * BLK, BLK), BLK), :] = turn(kv[:64], b, scale_all[b]).T.astype(BF16)
        vt_scr[:64, cols] = (kv[64:] * scale_all[b]).astype(BF16)
        return carry

    vt_scr[64:, :] = jnp.ones_like(vt_scr[64:, :])
    lax.fori_loop(0, 13 + x, make_kv, 0)

    def make_q(zb, carry):
        b = zb * 4 + x
        q = jnp.dot(ut[:256, :], one_hot(b), preferred_element_type=F32)
        row = scale_all[b] * (math.log2(math.e) / math.sqrt(HD))
        for h in range(4):
            qt_scr[zb, :, h * BLK : (h + 1) * BLK] = turn(q[h * HD : (h + 1) * HD], b, row).astype(BF16)
        return carry

    lax.fori_loop(0, 4, make_q, 0)

    def scores(zb, i, h):
        keys = k_scr[pl.ds(pl.multiple_of(i * BLK, BLK), BLK), :]
        return jnp.dot(keys, qt_scr[zb, :, h * BLK : (h + 1) * BLK], preferred_element_type=F32)

    def soft(i, s, state):
        top, acc = state
        new_top = jnp.maximum(top, jnp.max(s, axis=0, keepdims=True))
        probs = jnp.exp2(s - new_top).astype(BF16)
        values = vt_scr[:, pl.ds(pl.multiple_of(i * BLK, BLK), BLK)]
        acc = acc * jnp.exp2(top - new_top) + jnp.dot(values, probs, preferred_element_type=F32)
        return new_top, acc

    def attend(zb):
        n = zb * 4 + x

        def one(i, carry):
            states, now = carry
            later = [scores(zb, i + 1, h) for h in range(4)]
            return [soft(i, now[h], states[h]) for h in range(4)], later

        def four(j, carry):
            for k in range(4):
                carry = one(j * 4 + k, carry)
            return carry

        carry = (
            [(jnp.full((1, BLK), masked_score, F32), jnp.zeros((80, BLK), F32)) for _ in range(4)],
            [scores(zb, 0, h) for h in range(4)],
        )
        carry = lax.fori_loop(0, zb, four, carry)
        states, now = lax.fori_loop(4 * zb, n, one, carry)
        rows = lax.broadcasted_iota(jnp.int32, (BLK, BLK), 0)
        cols = lax.broadcasted_iota(jnp.int32, (BLK, BLK), 1)
        outs = []
        for h in range(4):
            _, acc = soft(n, jnp.where(rows <= cols, now[h], masked_score), states[h])
            outs.append((acc[:HD] / acc[HD : HD + 1]).astype(BF16))
        return jnp.concatenate(outs, axis=0)

    def att_copy(i, zb, slot):
        return rc(att_out.at[i], att_in.at[slot], at_s.at[i], at_r.at[i], (f, zb * 4 + x))

    def other_block(i, carry):
        zb = (zl + i) % 4
        att_out[i] = attend(zb)
        att_copy(i, zb, zl).start()
        return carry

    lax.fori_loop(1, 4, other_block, 0)

    for n, s in enumerate(steps):
        wo2_copy(n, s, (x - s + 4) % 4).wait_recv()
    rc(wo.at[:, :, core], wo.at[:, :, core], wo3_s.at[0], wo3_r.at[0], (sib, c)).start()

    att_in[zl] = attend(zl)

    ref = wo.at[:, :, 1 - core]
    rc(ref, ref, wo3_s.at[0], wo3_r.at[0], (sib, c)).wait_recv()
    for i in (1, 2, 3):
        slot = (zl - i + 4) % 4
        att_copy(i, slot, slot).wait_recv()

    attended = att_in[...].reshape(D, BLK)
    pick = (align_ref[...] - c * BLK == lax.broadcasted_iota(jnp.int32, (BLK, BLK), 0)).astype(BF16)
    total = jnp.zeros((BLK, 1), F32)
    for j in range(4):
        cols = pl.ds(j * 256, 256)
        branch = tn(attended, wo[j].reshape(D, 256))
        hidden = (lat_scr[:, cols].astype(F32) + branch).astype(BF16)
        hid_ref[:, cols] = hidden
        diff = tn(pick, hidden) - teach_ref[:, cols].astype(F32)
        total = total + jnp.sum(diff * diff, axis=1, keepdims=True)
    loss_ref[...] = jnp.broadcast_to(total * (1.0 / D), (BLK, 128)).T[0:1, :]

    loop(1, 8, lambda i: wc_copy(i, f % 8).wait_send())
    loop(1, 16, lambda i: ids_copy(i, c).wait_send())
    loop(1, 16, lambda i: wg_copy(i, g).wait_send())
    loop(1, 16, lambda i: wo_copy(i, g).wait_send())
    loop(1, 16, lambda i: sc_copy(i, c).wait_send())

    @pl.when(tap // 2 == core)
    def _():
        for step in (1, 2, 3):
            y_copy(step, tap).wait_send()

    for n, s in enumerate(steps):
        first_copy(n, z_dev(s), own).wait_send()
        ref = tt.at[:, x, :, half]
        rc(ref, ref, t4_s.at[n], t4_r.at[n], x_dev(s)).wait_send()
        wo2_copy(n, s, x).wait_send()
    for n in range(4):
        ref = tt.at[:, x, :, half]
        rc(ref, ref, t5_s.at[n], t5_r.at[n], (sib, c)).wait_send()
    rc(wg.at[:, core], wg.at[:, core], wgx_s.at[0], wgx_r.at[0], (sib, c)).wait_send()
    rc(wo.at[:, :, core], wo.at[:, :, core], wo3_s.at[0], wo3_r.at[0], (sib, c)).wait_send()
    for i in (1, 2, 3):
        att_copy(i, zl, zl).wait_send()


def body(byte_ids, byte_table, w_conv, w_qkv, w_out, norm_gain, teacher, align):
    f = lax.axis_index("fsdp")
    c = lax.axis_index("ctx")
    zl = c // 4
    ids = byte_ids[0].reshape(BLK, KW).T
    wc = lax.dynamic_slice_in_dim(w_conv, c * 64, 64, axis=1)
    wc = jnp.concatenate([wc[:48], wc[48:]], axis=1)
    wq = jnp.concatenate(
        [
            lax.dynamic_slice_in_dim(w_qkv, zl * 256, 256, axis=1),
            lax.dynamic_slice_in_dim(w_qkv, HQ * HD + zl * HD, HD, axis=1),
            lax.dynamic_slice_in_dim(w_qkv, (HQ + HK) * HD + zl * HD, HD, axis=1),
        ],
        axis=1,
    )
    gain = lax.dynamic_slice_in_dim(norm_gain, f * 32, 32, axis=0)
    wq = (wq.astype(F32) * gain.astype(F32)[:, None]).astype(BF16)
    cos, sin = rope_tables(NCTX * BLK)
    vm = pl.BlockSpec(memory_space=pltpu.VMEM)
    dma = pltpu.SemaphoreType.DMA
    hidden, loss = pl.pallas_call(
        kernel,
        out_shape=(
            jax.ShapeDtypeStruct((BLK, D), BF16),
            jax.ShapeDtypeStruct((1, BLK), F32),
        ),
        in_specs=[vm] * 9,
        out_specs=(vm, vm),
        scratch_shapes=[
            pltpu.VMEM((NCTX, KW, BLK), jnp.int32),
            pltpu.VMEM((NCTX, 1, BLK), F32),
            pltpu.VMEM((8, 48, 128), BF16),
            pltpu.VMEM((4, 4, 64, 1024), BF16),
            pltpu.VMEM((16, 2, 32, 384), BF16),
            pltpu.VMEM((4, 16, 2, 32, 256), BF16),
            pltpu.VMEM((384, 1024), BF16),
            pltpu.VMEM((NCTX * BLK, HD), BF16),
            pltpu.VMEM((80, NCTX * BLK), BF16),
            pltpu.VMEM((4, HD, 4 * BLK), BF16),
            pltpu.VMEM((BLK, D), BF16),
            pltpu.VMEM((4, BLK, BLK), BF16),
            pltpu.VMEM((4, BLK, BLK), BF16),
        ]
        + [
            dma((n,))
            for n in (16, 16, 16, 16, 8, 8, 4, 4, 3, 3, 3, 3, 4, 4, 16, 16, 1, 1, 16, 16, 3, 3, 1, 1, 4, 4)
        ],
        compiler_params=pltpu.CompilerParams(
            collective_id=0, has_side_effects=True, vmem_limit_bytes=56 * 2**20
        ),
    )(ids, byte_table, wc, wq, w_out, jnp.asarray(cos), jnp.asarray(sin), teacher[0], align)
    return hidden[None], loss


def solution(mesh):
    in_specs = (
        P("fsdp", "ctx"),
        P(),
        P("fsdp", None),
        P("fsdp", None),
        P("fsdp", None),
        P(),
        P("fsdp", "ctx", None),
        P("fsdp", "ctx"),
    )
    out_specs = (P("fsdp", "ctx", None), P("fsdp", "ctx"))
    return jax.shard_map(body, mesh=mesh, in_specs=in_specs, out_specs=out_specs, check_vma=False)
```

```python
import math

import jax
import jax.numpy as jnp
import numpy as np
from jax import lax
from jax.experimental import pallas as pl
from jax.experimental.pallas import tpu as pltpu
from jax.sharding import PartitionSpec as P

KW = 4
HQ = 16
HK = 4
HD = 64
D = 1024
BLK = 256
NCTX = 16
theta_base = 500000.0
norm_eps = 1e-05
masked_score = -1e30
MESH = pl.DeviceIdType.MESH
F32 = jnp.float32
BF16 = jnp.bfloat16


def rope_tables(length):
    half = HD // 2
    frequency = theta_base ** (-np.arange(half, dtype=np.float64) * 2.0 / HD)
    angles = frequency[:, None] * np.arange(length, dtype=np.float64)[None, :]
    return np.cos(angles).astype(np.float32), np.sin(angles).astype(np.float32)


def rc(src, dst, send, recv, dev):
    return pltpu.make_async_remote_copy(
        src_ref=src, dst_ref=dst, send_sem=send, recv_sem=recv, device_id=dev, device_id_type=MESH
    )


def tn(a, b):
    return lax.dot_general(a, b, (((0,), (0,)), ((), ())), preferred_element_type=F32)


def kernel(
    ids_ref, bt_ref, wconv_ref, wqkv_ref, wo_ref, gain_ref, cos_ref, sin_ref, teach_ref, align_ref,
    hid_ref, loss_ref,
    wc_src, wq_src, ids_all, scale_all, wc_all, tt, wg, wo, ut, k_scr, vt_scr, qt_scr, lat_scr, att_out, att_in,
    gain_scr, hot, raw_kv, raw_q,
    ids_s, ids_r, sc_s, sc_r, wc_s, wc_r, ty_s, ty_r, t3_s, t3_r, t4_s, t4_r, t5_s, t5_r,
    wg_s, wg_r, wgx_s, wgx_r, wo_s, wo_r, wo2_s, wo2_r, wo3_s, wo3_r, at_s, at_r,
):
    f = lax.axis_index("fsdp")
    c = lax.axis_index("ctx")
    core = f % 2
    y, zh = f // 4, (f // 2) % 2
    zl, x = c // 4, c % 4
    tap = f // 8
    sib = (f // 2) * 2 + 1 - core
    zfull = zh * 4 + zl
    steps = (1, -1, 2)

    def loop(lo, hi, fn):
        def step(i, carry):
            fn(i)
            return carry

        lax.fori_loop(lo, hi, step, 0)

    def ctx_peer(i):
        return (f, (c + i) % NCTX)

    def y_peer(i):
        return (((y + i) % 8) * 4 + zh * 2 + core, c)

    def mate_row(d):
        return y - y % 2 + (y + d // 2) % 2

    def block_dev(step, d):
        z2 = (zfull + step + 8) % 8
        return (mate_row(d) * 4 + (z2 // 4) * 2 + (core + d) % 2, (z2 % 4) * 4 + x)

    def z_dev(step):
        return block_dev(step, 0)

    def x_dev(step):
        return (f, zl * 4 + (x + step + 4) % 4)

    barrier = pltpu.get_barrier_semaphore()

    def sig(dev):
        pl.semaphore_signal(barrier, inc=1, device_id=dev, device_id_type=MESH)

    for d in range(4):
        for step in (1, -1, 2, -2):
            sig(block_dev(step, d))
    for d in range(1, 4):
        sig(block_dev(0, d))
    loop(1, 8, lambda i: sig(y_peer(i)))
    loop(1, 16, lambda i: sig(ctx_peer(i)))

    reach = jnp.where(zl == 3, 1, -1)
    at_edge = (zl == 3) | (zl == 0)
    gain_scr[...] = jnp.broadcast_to(
        gain_ref[:, pl.ds(pl.multiple_of(f // 4 * 128, 128), 128)].astype(F32), (128, 128)
    ).T
    my_gain = gain_scr[pl.ds(pl.multiple_of(f % 4 * 32, 32), 32), 0:1]

    def pack(slot, z):
        col = z * 4 + x
        both = wconv_ref[:, pl.ds(pl.multiple_of(col // 2 * 128, 128), 128)]
        mine = jnp.where(col % 2 == 0, both[:, :64], both[:, 64:])
        wc_src[slot] = jnp.concatenate([mine[:48], mine[48:]], axis=1)

        def heads_of(start):
            two = wqkv_ref[:, pl.ds(pl.multiple_of(start + z // 2 * 128, 128), 128)]
            return jnp.where(z % 2 == 0, two[:, :64], two[:, 64:])

        mine = jnp.concatenate(
            [wqkv_ref[:, pl.ds(pl.multiple_of(z * 256, 256), 256)], heads_of(HQ * HD), heads_of((HQ + HK) * HD)],
            axis=1,
        )
        wq_src[slot] = (mine.astype(F32) * my_gain).astype(BF16)

    pack(0, zl)
    for t in (1, 2):
        pack(t, (zl + reach * t + 4) % 4)

    def mate_slot(d, half_z):
        return (y + d // 2) % 2 * 4 + half_z * 2 + (core + d) % 2

    my_slot = mate_slot(0, zh)
    wc_all[my_slot] = wc_src[0]
    ids_all[c] = ids_ref[...]
    wg[y * 2 + zh, core] = wq_src[0]

    def quarter(z):
        return jnp.where(core == 0, x, z)

    def wo_cols(z):
        return wo_ref.at[:, pl.ds(pl.multiple_of(quarter(z) * 256, 256), 256)]

    my_quarter = quarter(zl)
    wo[my_quarter, y * 2 + zh, core] = wo_ref[:, pl.ds(pl.multiple_of(my_quarter * 256, 256), 256)]
    pl.semaphore_wait(barrier, 16 + 3 + 7 + 15)

    def wc_copy(d, slot):
        return rc(wc_src.at[0], wc_all.at[slot], wc_s.at[d], wc_r.at[d], block_dev(0, d))

    def wc_near(t, d, slot):
        return rc(
            wc_src.at[t], wc_all.at[slot], wc_s.at[4 * t + d], wc_r.at[4 + d], block_dev(reach * t, d)
        )

    def wq_near(t, slot):
        return rc(wq_src.at[t], wg.at[slot, core], wg_s.at[15 + t], wg_r.at[16], z_dev(reach * t))

    def wo_near(t, slot):
        z = (zl + reach * t + 4) % 4
        return rc(wo_cols(z), wo.at[quarter(z), slot, core], wo_s.at[15 + t], wo_r.at[16], z_dev(reach * t))

    @pl.when(at_edge)
    def _():
        for t in (1, 2):
            for d in range(4):
                wc_near(t, d, my_slot).start()

    for d in range(1, 4):
        wc_copy(d, my_slot).start()

    @pl.when(at_edge)
    def _():
        for t in (1, 2):
            wq_near(t, y * 2 + zh).start()
            wo_near(t, y * 2 + zh).start()

    def ids_copy(i, slot):
        return rc(ids_ref, ids_all.at[slot], ids_s.at[i], ids_r.at[i], ctx_peer(i))

    loop(1, 16, lambda i: ids_copy(i, c).start())

    def wg_copy(i, row, half_z):
        ref = wg.at[row * 2 + half_z, core]
        n = i + 8 * jnp.where(half_z == zh, 0, 1)
        return rc(ref, ref, wg_s.at[n], wg_r.at[n], y_peer(i))

    def wo_copy(i, row, half_z):
        ref = wo.at[my_quarter, row * 2 + half_z, core]
        n = i + 8 * jnp.where(half_z == zh, 0, 1)
        return rc(ref, ref, wo_s.at[n], wo_r.at[n], y_peer(i))

    loop(1, 8, lambda i: wg_copy(i, y, zh).start())

    btt = bt_ref[...].T
    bta = jnp.concatenate([btt[m * 96 : m * 96 + 48] for m in range(8)], axis=0)
    btb = jnp.concatenate([btt[m * 96 + 48 : m * 96 + 96] for m in range(8)], axis=0)

    for d in range(1, 4):
        wc_copy(d, mate_slot(d, zh)).wait_recv()
    for d in range(4):
        wc_near(1, d, mate_slot(d, 1 - zh)).wait_recv()
    wc_val = wc_all[...].reshape(384, 128)
    piece = tn(wc_val, bta)[:64] + tn(wc_val, btb)[64:]
    half = pl.ds(pl.multiple_of(core * 512, 512), 512)

    def y_copy(step, from_tap):
        ref = tt.at[zl, x, :, pl.ds(pl.multiple_of(from_tap * 256, 256), 256)]
        return rc(ref, ref, ty_s.at[step], ty_r.at[step], y_peer(2 * step))

    @pl.when(tap // 2 == core)
    def _():
        tt[zl, x, :, pl.ds(pl.multiple_of(tap * 256, 256), 256)] = piece.astype(BF16)
        for step in (1, 2, 3):
            y_copy(step, tap).start()

    wq_near(1, y * 2 + 1 - zh).wait_recv()
    loop(1, 8, lambda i: wg_copy(i, y, 1 - zh).start())

    for step in (1, 2, 3):
        src_tap = (tap - step + 4) % 4

        @pl.when(src_tap // 2 == core)
        def _():
            y_copy(step, src_tap).wait_recv()

    own = tt.at[zl, x, :, half]

    def first_copy(n, dev, ref):
        return rc(ref, ref, t3_s.at[n], t3_r.at[n], dev)

    @pl.when(core == 0)
    def _():
        for n, s in enumerate(steps):
            first_copy(n, z_dev(s), own).start()
        for n, s in enumerate(steps):
            first_copy(n, z_dev(s), tt.at[(zl - s + 4) % 4, x, :, half]).wait_recv()
        for n, s in enumerate(steps):
            ref = tt.at[:, x, :, half]
            rc(ref, ref, t4_s.at[n], t4_r.at[n], x_dev(s)).start()

    @pl.when(core == 1)
    def _():
        for n, s in enumerate(steps):
            first_copy(n, x_dev(s), own).start()
        for n, s in enumerate(steps):
            first_copy(n, x_dev(s), tt.at[zl, (x - s + 4) % 4, :, half]).wait_recv()
        for n, s in enumerate(steps):
            ref = tt.at[zl, :, :, half]
            rc(ref, ref, t4_s.at[n], t4_r.at[n], z_dev(s)).start()

    loop(1, 8, lambda i: wo_copy(i, y, zh).start())
    rc(
        wo_cols(zl), wo.at[my_quarter, y * 2 + 1 - zh, core], wo_s.at[16], wo_r.at[16], z_dev(1)
    ).wait_recv()
    loop(1, 8, lambda i: wo_copy(i, y, 1 - zh).start())

    def make_hot(b, carry):
        rows = lax.broadcasted_iota(jnp.int32, (256, BLK), 0)
        block = ids_all[b]
        for k in range(KW):
            hot[b, k * 256 : (k + 1) * 256] = (block[k : k + 1, :] == rows).astype(BF16)
        return carry

    loop(1, 16, lambda i: ids_copy(i, (c - i + NCTX) % NCTX).wait_recv())
    lax.fori_loop(0, 13 + x, make_hot, 0)

    @pl.when(core == 0)
    def _():
        ref = tt.at[:, x, :, half]
        rc(ref, ref, t5_s.at[0], t5_r.at[0], (sib, c)).start()
        for n, s in enumerate(steps):
            ref = tt.at[:, (x - s + 4) % 4, :, half]
            rc(ref, ref, t4_s.at[n], t4_r.at[n], x_dev(s)).wait_recv()
            rc(ref, ref, t5_s.at[n + 1], t5_r.at[n + 1], (sib, c)).start()
        other = pl.ds(512, 512)
        for n, s in enumerate((0,) + steps):
            ref = tt.at[(zl - s + 4) % 4, :, :, other]
            rc(ref, ref, t5_s.at[n], t5_r.at[n], (sib, c)).wait_recv()

    @pl.when(core == 1)
    def _():
        ref = tt.at[zl, :, :, half]
        rc(ref, ref, t5_s.at[0], t5_r.at[0], (sib, c)).start()
        for n, s in enumerate(steps):
            ref = tt.at[(zl - s + 4) % 4, :, :, half]
            rc(ref, ref, t4_s.at[n], t4_r.at[n], z_dev(s)).wait_recv()
            rc(ref, ref, t5_s.at[n + 1], t5_r.at[n + 1], (sib, c)).start()
        other = pl.ds(0, 512)
        for n, s in enumerate((0,) + steps):
            ref = tt.at[:, (x - s + 4) % 4, :, other]
            rc(ref, ref, t5_s.at[n], t5_r.at[n], (sib, c)).wait_recv()

    for half_z in (0, 1):
        loop(1, 8, lambda i: wg_copy(i, (y - i + 8) % 8, half_z).wait_recv())
    rc(wg.at[:, core], wg.at[:, core], wgx_s.at[0], wgx_r.at[0], (sib, c)).start()

    tall = tt[...].reshape(D, D)
    latent = jnp.dot(tall, hot[c], preferred_element_type=F32).astype(BF16)
    wide = latent.astype(F32)
    scale = lax.rsqrt(jnp.sum(wide * wide, axis=0, keepdims=True) * (1.0 / D) + norm_eps)
    scale_all[c] = scale

    def sc_copy(i, slot):
        ref = scale_all.at[slot]
        return rc(ref, ref, sc_s.at[i], sc_r.at[i], ctx_peer(i))

    loop(1, 16, lambda i: sc_copy(i, c).start())
    lat_scr[...] = latent.T

    ref = wg.at[:, 1 - core]
    rc(ref, ref, wgx_s.at[0], wgx_r.at[0], (sib, c)).wait_recv()
    ut[...] = tn(wg[...].reshape(D, 384), tall).astype(BF16)

    for half_z in (0, 1):
        loop(1, 8, lambda i: wo_copy(i, (y - i + 8) % 8, half_z).wait_recv())

    def wo2_copy(n, dev, slot):
        ref = wo.at[slot, :, core]
        return rc(ref, ref, wo2_s.at[n], wo2_r.at[n], dev)

    @pl.when(core == 0)
    def _():
        for n, s in enumerate(steps):
            wo2_copy(n, x_dev(s), my_quarter).start()

    @pl.when(core == 1)
    def _():
        for n, s in enumerate(steps):
            wo2_copy(n, z_dev(s), my_quarter).start()

    def make_kv(b, carry):
        raw_kv[b] = jnp.dot(ut[256:384, :], hot[b], preferred_element_type=F32)
        return carry

    def make_q(zb, carry):
        raw_q[zb] = jnp.dot(ut[:256, :], hot[zb * 4 + x], preferred_element_type=F32)
        return carry

    lax.fori_loop(0, 13 + x, make_kv, 0)
    lax.fori_loop(0, 4, make_q, 0)
    loop(1, 16, lambda i: sc_copy(i, (c - i + NCTX) % NCTX).wait_recv())

    def turn(v, b, scale_row):
        cols = pl.ds(pl.multiple_of(b * BLK, BLK), BLK)
        cos, sin = cos_ref[:, cols] * scale_row, sin_ref[:, cols] * scale_row
        lo, hi = v[:32], v[32:]
        return jnp.concatenate([lo * cos - hi * sin, hi * cos + lo * sin], axis=0)

    def turn_kv(b, carry):
        cols = pl.ds(pl.multiple_of(b * BLK, BLK), BLK)
        k_scr[pl.ds(pl.multiple_of(b * BLK, BLK), BLK), :] = (
            turn(raw_kv[b, :64], b, scale_all[b]).astype(BF16).T
        )
        vt_scr[:64, cols] = (raw_kv[b, 64:] * scale_all[b]).astype(BF16)
        return carry

    def turn_q(zb, carry):
        b = zb * 4 + x
        row = scale_all[b] * (math.log2(math.e) / math.sqrt(HD))
        for h in range(4):
            qt_scr[zb, :, h * BLK : (h + 1) * BLK] = turn(raw_q[zb, h * HD : (h + 1) * HD], b, row).astype(BF16)
        return carry

    vt_scr[64:, :] = jnp.ones_like(vt_scr[64:, :])
    lax.fori_loop(0, 13 + x, turn_kv, 0)
    lax.fori_loop(0, 4, turn_q, 0)

    def scores(zb, i, h):
        keys = k_scr[pl.ds(pl.multiple_of(i * BLK, BLK), BLK), :]
        return jnp.dot(keys, qt_scr[zb, :, h * BLK : (h + 1) * BLK], preferred_element_type=F32)

    def soft(i, s, state):
        top, acc = state
        new_top = jnp.maximum(top, jnp.max(s, axis=0, keepdims=True))
        probs = jnp.exp2(s - new_top).astype(BF16)
        values = vt_scr[:, pl.ds(pl.multiple_of(i * BLK, BLK), BLK)]
        acc = acc * jnp.exp2(top - new_top) + jnp.dot(values, probs, preferred_element_type=F32)
        return new_top, acc

    def attend(zb):
        n = zb * 4 + x

        def one(i, carry):
            states, now = carry
            later = [scores(zb, i + 1, h) for h in range(4)]
            return [soft(i, now[h], states[h]) for h in range(4)], later

        def four(j, carry):
            for k in range(4):
                carry = one(j * 4 + k, carry)
            return carry

        carry = (
            [(jnp.full((1, BLK), masked_score, F32), jnp.zeros((80, BLK), F32)) for _ in range(4)],
            [scores(zb, 0, h) for h in range(4)],
        )
        carry = lax.fori_loop(0, zb, four, carry)
        states, now = lax.fori_loop(4 * zb, n, one, carry)
        rows = lax.broadcasted_iota(jnp.int32, (BLK, BLK), 0)
        cols = lax.broadcasted_iota(jnp.int32, (BLK, BLK), 1)
        outs = []
        for h in range(4):
            _, acc = soft(n, jnp.where(rows <= cols, now[h], masked_score), states[h])
            outs.append((acc[:HD] / acc[HD : HD + 1]).astype(BF16))
        return jnp.concatenate(outs, axis=0)

    def att_copy(i, zb, slot):
        return rc(att_out.at[i], att_in.at[slot], at_s.at[i], at_r.at[i], (f, zb * 4 + x))

    def other_block(i, carry):
        zb = (zl + i) % 4
        att_out[i] = attend(zb)
        att_copy(i, zb, zl).start()
        return carry

    lax.fori_loop(1, 4, other_block, 0)

    for n, s in enumerate(steps):
        wo2_copy(n, x_dev(s), (my_quarter - s + 4) % 4).wait_recv()
    rc(wo.at[:, :, core], wo.at[:, :, core], wo3_s.at[0], wo3_r.at[0], (sib, c)).start()

    att_in[zl] = attend(zl)

    ref = wo.at[:, :, 1 - core]
    rc(ref, ref, wo3_s.at[0], wo3_r.at[0], (sib, c)).wait_recv()
    for i in (1, 2, 3):
        slot = (zl - i + 4) % 4
        att_copy(i, slot, slot).wait_recv()

    attended = att_in[...].reshape(D, BLK)
    pick = (align_ref[...] - c * BLK == lax.broadcasted_iota(jnp.int32, (BLK, BLK), 0)).astype(BF16)
    total = jnp.zeros((BLK, 1), F32)
    for j in range(4):
        cols = pl.ds(j * 256, 256)
        branch = tn(attended, wo[j].reshape(D, 256))
        hidden = (lat_scr[:, cols].astype(F32) + branch).astype(BF16)
        hid_ref[:, cols] = hidden
        diff = tn(pick, hidden) - teach_ref[:, cols].astype(F32)
        total = total + jnp.sum(diff * diff, axis=1, keepdims=True)
    loss_ref[...] = jnp.broadcast_to(total * (1.0 / D), (BLK, 128)).T[0:1, :]

    for d in range(1, 4):
        wc_copy(d, my_slot).wait_send()

    @pl.when(at_edge)
    def _():
        for t in (1, 2):
            for d in range(4):
                wc_near(t, d, my_slot).wait_send()
            wq_near(t, y * 2 + zh).wait_send()
            wo_near(t, y * 2 + zh).wait_send()

    loop(1, 16, lambda i: ids_copy(i, c).wait_send())
    loop(1, 16, lambda i: sc_copy(i, c).wait_send())
    for half_z in (0, 1):
        loop(1, 8, lambda i: wg_copy(i, y, half_z).wait_send())
        loop(1, 8, lambda i: wo_copy(i, y, half_z).wait_send())

    @pl.when(tap // 2 == core)
    def _():
        for step in (1, 2, 3):
            y_copy(step, tap).wait_send()

    for n, s in enumerate(steps):
        first_copy(n, z_dev(s), own).wait_send()
        ref = tt.at[:, x, :, half]
        rc(ref, ref, t4_s.at[n], t4_r.at[n], x_dev(s)).wait_send()
        wo2_copy(n, x_dev(s), my_quarter).wait_send()
    for n in range(4):
        ref = tt.at[:, x, :, half]
        rc(ref, ref, t5_s.at[n], t5_r.at[n], (sib, c)).wait_send()
    rc(wg.at[:, core], wg.at[:, core], wgx_s.at[0], wgx_r.at[0], (sib, c)).wait_send()
    rc(wo.at[:, :, core], wo.at[:, :, core], wo3_s.at[0], wo3_r.at[0], (sib, c)).wait_send()
    for i in (1, 2, 3):
        att_copy(i, zl, zl).wait_send()


def body(byte_ids, byte_table, w_conv, w_qkv, w_out, norm_gain, teacher, align):
    ids = byte_ids[0].reshape(BLK, KW).T
    cos, sin = rope_tables(NCTX * BLK)
    vm = pl.BlockSpec(memory_space=pltpu.VMEM)
    dma = pltpu.SemaphoreType.DMA
    hidden, loss = pl.pallas_call(
        kernel,
        out_shape=(
            jax.ShapeDtypeStruct((BLK, D), BF16),
            jax.ShapeDtypeStruct((1, BLK), F32),
        ),
        in_specs=[vm] * 10,
        out_specs=(vm, vm),
        scratch_shapes=[
            pltpu.VMEM((3, 48, 128), BF16),
            pltpu.VMEM((3, 32, 384), BF16),
            pltpu.VMEM((NCTX, KW, BLK), jnp.int32),
            pltpu.VMEM((NCTX, 1, BLK), F32),
            pltpu.VMEM((8, 48, 128), BF16),
            pltpu.VMEM((4, 4, 64, 1024), BF16),
            pltpu.VMEM((16, 2, 32, 384), BF16),
            pltpu.VMEM((4, 16, 2, 32, 256), BF16),
            pltpu.VMEM((384, 1024), BF16),
            pltpu.VMEM((NCTX * BLK, HD), BF16),
            pltpu.VMEM((80, NCTX * BLK), BF16),
            pltpu.VMEM((4, HD, 4 * BLK), BF16),
            pltpu.VMEM((BLK, D), BF16),
            pltpu.VMEM((4, BLK, BLK), BF16),
            pltpu.VMEM((4, BLK, BLK), BF16),
            pltpu.VMEM((128, 128), F32),
            pltpu.VMEM((NCTX, D, BLK), BF16),
            pltpu.VMEM((NCTX, 128, BLK), F32),
            pltpu.VMEM((4, BLK, BLK), F32),
        ]
        + [
            dma((n,))
            for n in (16, 16, 16, 16, 12, 8, 4, 4, 3, 3, 3, 3, 4, 4, 18, 17, 1, 1, 18, 17, 3, 3, 1, 1, 4, 4)
        ],
        compiler_params=pltpu.CompilerParams(
            collective_id=0, has_side_effects=True, vmem_limit_bytes=56 * 2**20
        ),
    )(ids, byte_table, w_conv, w_qkv, w_out, norm_gain[None], jnp.asarray(cos), jnp.asarray(sin), teacher[0], align)
    return hidden[None], loss


def solution(mesh):
    in_specs = (
        P("fsdp", "ctx"),
        P(),
        P("fsdp", None),
        P("fsdp", None),
        P("fsdp", None),
        P(),
        P("fsdp", "ctx", None),
        P("fsdp", "ctx"),
    )
    out_specs = (P("fsdp", "ctx", None), P("fsdp", "ctx"))
    return jax.shard_map(body, mesh=mesh, in_specs=in_specs, out_specs=out_specs, check_vma=False)
```

```python
import math

import jax
import jax.numpy as jnp
import numpy as np
from jax import lax
from jax.experimental import pallas as pl
from jax.experimental.pallas import tpu as pltpu
from jax.sharding import PartitionSpec as P

KW = 4
HQ = 16
HK = 4
HD = 64
D = 1024
BLK = 256
NCTX = 16
theta_base = 500000.0
norm_eps = 1e-05
masked_score = -1e30
MESH = pl.DeviceIdType.MESH
F32 = jnp.float32
BF16 = jnp.bfloat16


def rope_tables(length):
    half = HD // 2
    frequency = theta_base ** (-np.arange(half, dtype=np.float64) * 2.0 / HD)
    angles = frequency[:, None] * np.arange(length, dtype=np.float64)[None, :]
    return np.cos(angles).astype(np.float32), np.sin(angles).astype(np.float32)


def rc(src, dst, send, recv, dev):
    return pltpu.make_async_remote_copy(
        src_ref=src, dst_ref=dst, send_sem=send, recv_sem=recv, device_id=dev, device_id_type=MESH
    )


def tn(a, b):
    return lax.dot_general(a, b, (((0,), (0,)), ((), ())), preferred_element_type=F32)


def kernel(
    ids_ref, bt_ref, wconv_ref, wqkv_ref, wo_ref, gain_ref, cos_hbm, sin_hbm, teach_hbm, align_ref,
    hid_ref, loss_ref,
    wc_src, wq_src, ids_all, scale_all, wc_all, tt, wg, wo, ut, k_scr, vt_scr, qt_scr, lat_scr, att_out, att_in,
    gain_scr, hot, raw_kv, raw_q, lat_acc, cos_ref, sin_ref, teach_ref, in_s,
    ids_s, ids_r, sc_s, sc_r, wc_s, wc_r, ty_s, ty_r, t3_s, t3_r, t4_s, t4_r, t5_s, t5_r,
    wg_s, wg_r, wgx_s, wgx_r, wo_s, wo_r, wo2_s, wo2_r, wo3_s, wo3_r, at_s, at_r,
):
    f = lax.axis_index("fsdp")
    c = lax.axis_index("ctx")
    core = f % 2
    y, zh = f // 4, (f // 2) % 2
    zl, x = c // 4, c % 4
    tap = f // 8
    sib = (f // 2) * 2 + 1 - core
    zfull = zh * 4 + zl
    steps = (1, -1, 2)

    def loop(lo, hi, fn):
        def step(i, carry):
            fn(i)
            return carry

        lax.fori_loop(lo, hi, step, 0)

    def ctx_peer(i):
        return (f, (c + i) % NCTX)

    def y_peer(i):
        return (((y + i) % 8) * 4 + zh * 2 + core, c)

    def mate_row(d):
        return y - y % 2 + (y + d // 2) % 2

    def block_dev(step, d):
        z2 = (zfull + step + 8) % 8
        return (mate_row(d) * 4 + (z2 // 4) * 2 + (core + d) % 2, (z2 % 4) * 4 + x)

    def z_dev(step):
        return block_dev(step, 0)

    def x_dev(step):
        return (f, zl * 4 + (x + step + 4) % 4)

    barrier = pltpu.get_barrier_semaphore()

    def sig(dev):
        pl.semaphore_signal(barrier, inc=1, device_id=dev, device_id_type=MESH)

    for d in range(4):
        for step in (1, -1, 2, -2):
            sig(block_dev(step, d))
    for d in range(1, 4):
        sig(block_dev(0, d))
    loop(1, 8, lambda i: sig(y_peer(i)))
    loop(1, 16, lambda i: sig(ctx_peer(i)))

    reach = jnp.where(zl == 3, 1, -1)
    at_edge = (zl == 3) | (zl == 0)

    def pack_conv(slot, z):
        col = z * 4 + x
        both = wconv_ref[:, pl.ds(pl.multiple_of(col // 2 * 128, 128), 128)]
        mine = jnp.where(col % 2 == 0, both[:, :64], both[:, 64:])
        wc_src[slot] = jnp.concatenate([mine[:48], mine[48:]], axis=1)

    def mate_slot(d, half_z):
        return (y + d // 2) % 2 * 4 + half_z * 2 + (core + d) % 2

    my_slot = mate_slot(0, zh)
    pack_conv(0, zl)
    for t in (1, 2):
        pack_conv(t, (zl + reach * t + 4) % 4)
    wc_all[my_slot] = wc_src[0]
    pl.semaphore_wait(barrier, 16 + 3 + 7 + 15)

    def wc_copy(d, slot):
        return rc(wc_src.at[0], wc_all.at[slot], wc_s.at[d], wc_r.at[d], block_dev(0, d))

    def wc_near(t, d, slot):
        return rc(
            wc_src.at[t], wc_all.at[slot], wc_s.at[4 * t + d], wc_r.at[4 + d], block_dev(reach * t, d)
        )

    @pl.when(at_edge)
    def _():
        for t in (1, 2):
            for d in range(4):
                wc_near(t, d, my_slot).start()

    for d in range(1, 4):
        wc_copy(d, my_slot).start()

    late = [
        pltpu.make_async_copy(src, dst, in_s.at[n])
        for n, (src, dst) in enumerate(((cos_hbm, cos_ref), (sin_hbm, sin_ref), (teach_hbm, teach_ref)))
    ]
    for copy in late:
        copy.start()

    taps = lax.broadcasted_iota(jnp.int32, (8, 4 * BLK), 0)
    at = lax.broadcasted_iota(jnp.int32, (8, 4 * BLK), 1)
    spread = jnp.where(at % KW == taps, jnp.broadcast_to(ids_ref[...], (8, 4 * BLK)).astype(F32), 0.0)
    to_row = lax.broadcasted_iota(jnp.int32, (4 * BLK, BLK), 0) // KW
    to_row = (to_row == lax.broadcasted_iota(jnp.int32, (4 * BLK, BLK), 1)).astype(BF16)
    rows_of = jnp.dot(spread.astype(BF16), to_row, preferred_element_type=F32)
    ids_all[c] = rows_of[:KW].astype(jnp.int32)

    def ids_copy(i, slot):
        ref = ids_all.at[slot]
        return rc(ref, ref, ids_s.at[i], ids_r.at[i], ctx_peer(i))

    gains = gain_ref[...].astype(F32)
    here = lax.broadcasted_iota(jnp.int32, (8, 128), 0) == f // 4
    gains = jnp.sum(jnp.where(here, gains, 0.0), axis=0, keepdims=True)
    gain_scr[...] = jnp.broadcast_to(gains, (128, 128)).T
    my_gain = gain_scr[pl.ds(pl.multiple_of(f % 4 * 32, 32), 32), 0:1]

    def pack_heads(slot, z):
        def heads_of(start):
            two = wqkv_ref[:, pl.ds(pl.multiple_of(start + z // 2 * 128, 128), 128)]
            return jnp.where(z % 2 == 0, two[:, :64], two[:, 64:])

        mine = jnp.concatenate(
            [wqkv_ref[:, pl.ds(pl.multiple_of(z * 256, 256), 256)], heads_of(HQ * HD), heads_of((HQ + HK) * HD)],
            axis=1,
        )
        wq_src[slot] = (mine.astype(F32) * my_gain).astype(BF16)

    pack_heads(0, zl)
    for t in (1, 2):
        pack_heads(t, (zl + reach * t + 4) % 4)
    wg[y * 2 + zh, core] = wq_src[0]

    def quarter(z):
        return jnp.where(core == 0, x, z)

    def wo_cols(z):
        return wo_ref.at[:, pl.ds(pl.multiple_of(quarter(z) * 256, 256), 256)]

    my_quarter = quarter(zl)
    wo[my_quarter, y * 2 + zh, core] = wo_ref[:, pl.ds(pl.multiple_of(my_quarter * 256, 256), 256)]

    def wq_near(t, slot):
        return rc(wq_src.at[t], wg.at[slot, core], wg_s.at[15 + t], wg_r.at[16], z_dev(reach * t))

    def wo_near(t, slot):
        z = (zl + reach * t + 4) % 4
        return rc(wo_cols(z), wo.at[quarter(z), slot, core], wo_s.at[15 + t], wo_r.at[16], z_dev(reach * t))

    @pl.when(at_edge)
    def _():
        for t in (1, 2):
            wq_near(t, y * 2 + zh).start()
            wo_near(t, y * 2 + zh).start()

    loop(1, 16, lambda i: ids_copy(i, c).start())

    def wg_copy(i, row, half_z):
        ref = wg.at[row * 2 + half_z, core]
        n = i + 8 * jnp.where(half_z == zh, 0, 1)
        return rc(ref, ref, wg_s.at[n], wg_r.at[n], y_peer(i))

    def wo_copy(i, row, half_z):
        ref = wo.at[my_quarter, row * 2 + half_z, core]
        n = i + 8 * jnp.where(half_z == zh, 0, 1)
        return rc(ref, ref, wo_s.at[n], wo_r.at[n], y_peer(i))

    loop(1, 8, lambda i: wg_copy(i, y, zh).start())

    btt = bt_ref[...].T
    bta = jnp.concatenate([btt[m * 96 : m * 96 + 48] for m in range(8)], axis=0)
    btb = jnp.concatenate([btt[m * 96 + 48 : m * 96 + 96] for m in range(8)], axis=0)

    for d in range(1, 4):
        wc_copy(d, mate_slot(d, zh)).wait_recv()
    for d in range(4):
        wc_near(1, d, mate_slot(d, 1 - zh)).wait_recv()
    wc_val = wc_all[...].reshape(384, 128)
    piece = tn(wc_val, bta)[:64] + tn(wc_val, btb)[64:]

    away = jnp.where(y % 2 == 0, -1, 1)

    def y_copy(step, from_tap):
        ref = tt.at[core, zl, x, :, pl.ds(pl.multiple_of(from_tap % 2 * 256, 256), 256)]
        return rc(ref, ref, ty_s.at[step], ty_r.at[step], y_peer(8 + away * step))

    @pl.when(tap // 2 == core)
    def _():
        tt[core, zl, x, :, pl.ds(pl.multiple_of(tap % 2 * 256, 256), 256)] = piece.astype(BF16)
        for step in (1, 2, 3):
            y_copy(step, tap).start()

    wq_near(1, y * 2 + 1 - zh).wait_recv()
    loop(1, 8, lambda i: wg_copy(i, y, 1 - zh).start())

    for step in (1, 2, 3):
        src_tap = (tap + (away, -away, 2)[step - 1] + 4) % 4

        @pl.when(src_tap // 2 == core)
        def _():
            y_copy(step, src_tap).wait_recv()

    own = tt.at[core, zl, x]

    def first_copy(n, dev, ref):
        return rc(ref, ref, t3_s.at[n], t3_r.at[n], dev)

    ways = (1, -1, 1, -1, 1, -1)
    parts = (0, 2, 2, 0, 0, 2)

    def along_x(n, shift):
        ref = tt.at[core, pl.ds(parts[n], 2), (x + shift + 4) % 4]
        return rc(ref, ref, t4_s.at[n], t4_r.at[n], x_dev(ways[n]))

    def along_z(n, shift):
        ref = tt.at[core, (zl + shift + 4) % 4, pl.ds(parts[n], 2)]
        return rc(ref, ref, t4_s.at[n], t4_r.at[n], z_dev(ways[n]))

    def over(n, ref):
        return rc(ref, ref, t5_s.at[n], t5_r.at[n], (sib, c))

    def second_axis(along, slice_of):
        over(0, slice_of(0, core)).start()
        along(0, -1).wait_recv()
        along(4, -1).start()
        along(1, 1).wait_recv()
        along(5, 1).start()
        along(2, -1).wait_recv()
        over(1, slice_of(-1, core)).start()
        along(3, 1).wait_recv()
        over(2, slice_of(1, core)).start()
        along(4, -2).wait_recv()
        along(5, 2).wait_recv()
        over(3, slice_of(2, core)).start()

    def slice_x(shift, part):
        return tt.at[part, :, (x + shift + 4) % 4]

    def slice_z(shift, part):
        return tt.at[part, (zl + shift + 4) % 4]

    @pl.when(core == 0)
    def _():
        for n, s in enumerate(steps):
            first_copy(n, z_dev(s), own).start()
        for n, s in enumerate(steps):
            first_copy(n, z_dev(s), tt.at[core, (zl - s + 4) % 4, x]).wait_recv()
        for n in (0, 1, 2, 3):
            along_x(n, 0).start()

    @pl.when(core == 1)
    def _():
        for n, s in enumerate(steps):
            first_copy(n, x_dev(s), own).start()
        for n, s in enumerate(steps):
            first_copy(n, x_dev(s), tt.at[core, zl, (x - s + 4) % 4]).wait_recv()
        for n in (0, 1, 2, 3):
            along_z(n, 0).start()

    loop(1, 8, lambda i: wo_copy(i, y, zh).start())
    rc(
        wo_cols(zl), wo.at[my_quarter, y * 2 + 1 - zh, core], wo_s.at[16], wo_r.at[16], z_dev(1)
    ).wait_recv()
    loop(1, 8, lambda i: wo_copy(i, y, 1 - zh).start())

    def make_hot(b, carry):
        rows = lax.broadcasted_iota(jnp.int32, (256, BLK), 0)
        block = ids_all[b]
        for k in range(KW):
            hot[b, k * 256 : (k + 1) * 256] = (block[k : k + 1, :] == rows).astype(BF16)
        return carry

    loop(1, 16, lambda i: ids_copy(i, (c - i + NCTX) % NCTX).wait_recv())
    lax.fori_loop(0, NCTX, make_hot, 0)

    @pl.when(core == 0)
    def _():
        second_axis(along_x, slice_x)

    @pl.when(core == 1)
    def _():
        second_axis(along_z, slice_z)

    for half_z in (0, 1):
        loop(1, 8, lambda i: wg_copy(i, (y - i + 8) % 8, half_z).wait_recv())
    rc(wg.at[:, core], wg.at[:, core], wgx_s.at[0], wgx_r.at[0], (sib, c)).start()

    def table(part):
        return tt[part].reshape(D, 512)

    def hot_rows(b, part):
        return hot[b, pl.ds(pl.multiple_of(part * 512, 512), 512)]

    lat_acc[...] = jnp.dot(table(core), hot_rows(c, core), preferred_element_type=F32)

    @pl.when(core == 0)
    def _():
        for n, shift in enumerate((0, -1, 1, 2)):
            over(n, slice_z(shift, 1 - core)).wait_recv()

    @pl.when(core == 1)
    def _():
        for n, shift in enumerate((0, -1, 1, 2)):
            over(n, slice_x(shift, 1 - core)).wait_recv()

    latent = lat_acc[...] + jnp.dot(table(1 - core), hot_rows(c, 1 - core), preferred_element_type=F32)
    latent = latent.astype(BF16)
    wide = latent.astype(F32)
    scale = lax.rsqrt(jnp.sum(wide * wide, axis=0, keepdims=True) * (1.0 / D) + norm_eps)
    scale_all[c] = scale

    def sc_copy(i, slot):
        ref = scale_all.at[slot]
        return rc(ref, ref, sc_s.at[i], sc_r.at[i], ctx_peer(i))

    loop(1, 16, lambda i: sc_copy(i, c).start())
    lat_scr[...] = latent.T

    ref = wg.at[:, 1 - core]
    rc(ref, ref, wgx_s.at[0], wgx_r.at[0], (sib, c)).wait_recv()
    wgt = wg[...].reshape(D, 384)
    for part in (0, 1):
        ut[:, part * 512 : (part + 1) * 512] = tn(wgt, table(part)).astype(BF16)

    for half_z in (0, 1):
        loop(1, 8, lambda i: wo_copy(i, (y - i + 8) % 8, half_z).wait_recv())

    def wo2_copy(n, dev, slot):
        ref = wo.at[slot, :, core]
        return rc(ref, ref, wo2_s.at[n], wo2_r.at[n], dev)

    @pl.when(core == 0)
    def _():
        for n, s in enumerate(steps):
            wo2_copy(n, x_dev(s), my_quarter).start()

    @pl.when(core == 1)
    def _():
        for n, s in enumerate(steps):
            wo2_copy(n, z_dev(s), my_quarter).start()

    def make_kv(b, carry):
        raw_kv[b] = jnp.dot(ut[256:384, :], hot[b], preferred_element_type=F32)
        return carry

    def make_q(zb, carry):
        raw_q[zb] = jnp.dot(ut[:256, :], hot[zb * 4 + x], preferred_element_type=F32)
        return carry

    lax.fori_loop(0, NCTX, make_kv, 0)
    lax.fori_loop(0, 4, make_q, 0)
    loop(1, 16, lambda i: sc_copy(i, (c - i + NCTX) % NCTX).wait_recv())

    def turn(v, b, scale_row):
        cols = pl.ds(pl.multiple_of(b * BLK, BLK), BLK)
        cos, sin = cos_ref[:, cols] * scale_row, sin_ref[:, cols] * scale_row
        lo, hi = v[:32], v[32:]
        return jnp.concatenate([lo * cos - hi * sin, hi * cos + lo * sin], axis=0)

    def turn_kv(b, carry):
        cols = pl.ds(pl.multiple_of(b * BLK, BLK), BLK)
        k_scr[pl.ds(pl.multiple_of(b * BLK, BLK), BLK), :] = (
            turn(raw_kv[b, :64], b, scale_all[b]).astype(BF16).T
        )
        vt_scr[:64, cols] = (raw_kv[b, 64:] * scale_all[b]).astype(BF16)
        return carry

    def turn_q(zb, carry):
        b = zb * 4 + x
        row = scale_all[b] * (math.log2(math.e) / math.sqrt(HD))
        for h in range(4):
            qt_scr[zb, :, h * BLK : (h + 1) * BLK] = turn(raw_q[zb, h * HD : (h + 1) * HD], b, row).astype(BF16)
        return carry

    vt_scr[64:, :] = jnp.ones_like(vt_scr[64:, :])
    for copy in late:
        copy.wait()
    lax.fori_loop(0, NCTX, turn_kv, 0)
    lax.fori_loop(0, 4, turn_q, 0)

    def scores(zb, i, h):
        keys = k_scr[pl.ds(pl.multiple_of(i * BLK, BLK), BLK), :]
        return jnp.dot(keys, qt_scr[zb, :, h * BLK : (h + 1) * BLK], preferred_element_type=F32)

    def soft(i, s, state):
        top, acc = state
        new_top = jnp.maximum(top, jnp.max(s, axis=0, keepdims=True))
        probs = jnp.exp2(s - new_top).astype(BF16)
        values = vt_scr[:, pl.ds(pl.multiple_of(i * BLK, BLK), BLK)]
        acc = acc * jnp.exp2(top - new_top) + jnp.dot(values, probs, preferred_element_type=F32)
        return new_top, acc

    key_row = lax.broadcasted_iota(jnp.int32, (BLK, BLK), 0)
    query_row = lax.broadcasted_iota(jnp.int32, (BLK, BLK), 1) + x * BLK

    def attend(zb):
        def one(i, carry, masked_block):
            states, now = carry
            later, new_states = [], []
            for h in range(4):
                if masked_block != 3:
                    later.append(scores(zb, i + 1, h))
                s = now[h]
                if masked_block is not None:
                    s = jnp.where(key_row + masked_block * BLK <= query_row, s, masked_score)
                new_states.append(soft(i, s, states[h]))
            return new_states, later

        def four(j, carry):
            for k in range(4):
                carry = one(j * 4 + k, carry, None)
            return carry

        carry = (
            [(jnp.full((1, BLK), masked_score, F32), jnp.zeros((80, BLK), F32)) for _ in range(4)],
            [scores(zb, 0, h) for h in range(4)],
        )
        carry = lax.fori_loop(0, zb, four, carry)
        for k in range(4):
            carry = one(4 * zb + k, carry, k)
        for h in range(4):
            _, acc = carry[0][h]
            att_out[zb, h * HD : (h + 1) * HD] = (acc[:HD] / acc[HD : HD + 1]).astype(BF16)

    def att_copy(zb, slot):
        return rc(att_out.at[zb], att_in.at[slot], at_s.at[zb], at_r.at[slot], (f, zb * 4 + x))

    def block_step(i, carry):
        zb = (zl + i) % 4

        @pl.when(i == 3)
        def _():
            for n, s in enumerate(steps):
                wo2_copy(n, x_dev(s), (my_quarter - s + 4) % 4).wait_recv()
            rc(wo.at[:, :, core], wo.at[:, :, core], wo3_s.at[0], wo3_r.at[0], (sib, c)).start()

        for k in range(4):

            @pl.when(zb == k)
            def _():
                attend(k)

        @pl.when(i < 4)
        def _():
            att_copy(zb, zl).start()

        return carry

    lax.fori_loop(1, 5, block_step, 0)
    att_in[zl] = att_out[zl]

    ref = wo.at[:, :, 1 - core]
    rc(ref, ref, wo3_s.at[0], wo3_r.at[0], (sib, c)).wait_recv()
    for i in (1, 2, 3):
        slot = (zl - i + 4) % 4
        att_copy(slot, slot).wait_recv()

    attended = att_in[...].reshape(D, BLK)
    pick = (align_ref[...] - c * BLK == lax.broadcasted_iota(jnp.int32, (BLK, BLK), 0)).astype(BF16)
    total = jnp.zeros((BLK, 1), F32)
    for j in range(4):
        cols = pl.ds(j * 256, 256)
        branch = tn(attended, wo[j].reshape(D, 256))
        hidden = (lat_scr[:, cols].astype(F32) + branch).astype(BF16)
        hid_ref[:, cols] = hidden
        diff = tn(pick, hidden) - teach_ref[:, cols].astype(F32)
        total = total + jnp.sum(diff * diff, axis=1, keepdims=True)
    loss_ref[...] = jnp.broadcast_to(total * (1.0 / D), (BLK, 128)).T[0:1, :]

    for d in range(1, 4):
        wc_copy(d, my_slot).wait_send()

    @pl.when(at_edge)
    def _():
        for t in (1, 2):
            for d in range(4):
                wc_near(t, d, my_slot).wait_send()
            wq_near(t, y * 2 + zh).wait_send()
            wo_near(t, y * 2 + zh).wait_send()

    loop(1, 16, lambda i: ids_copy(i, c).wait_send())
    loop(1, 16, lambda i: sc_copy(i, c).wait_send())
    for half_z in (0, 1):
        loop(1, 8, lambda i: wg_copy(i, y, half_z).wait_send())
        loop(1, 8, lambda i: wo_copy(i, y, half_z).wait_send())

    @pl.when(tap // 2 == core)
    def _():
        for step in (1, 2, 3):
            y_copy(step, tap).wait_send()

    for n, s in enumerate(steps):
        first_copy(n, z_dev(s), own).wait_send()
        wo2_copy(n, x_dev(s), my_quarter).wait_send()
    for n in range(6):
        along_x(n, 0).wait_send()
    for n in range(4):
        over(n, slice_x(0, core)).wait_send()
    rc(wg.at[:, core], wg.at[:, core], wgx_s.at[0], wgx_r.at[0], (sib, c)).wait_send()
    rc(wo.at[:, :, core], wo.at[:, :, core], wo3_s.at[0], wo3_r.at[0], (sib, c)).wait_send()
    for i in (1, 2, 3):
        att_copy((zl + i) % 4, zl).wait_send()


def body(byte_ids, byte_table, w_conv, w_qkv, w_out, norm_gain, teacher, align):
    cos, sin = rope_tables(NCTX * BLK)
    vm = pl.BlockSpec(memory_space=pltpu.VMEM)
    dma = pltpu.SemaphoreType.DMA
    hidden, loss = pl.pallas_call(
        kernel,
        out_shape=(
            jax.ShapeDtypeStruct((BLK, D), BF16),
            jax.ShapeDtypeStruct((1, BLK), F32),
        ),
        in_specs=[vm] * 6 + [pl.BlockSpec(memory_space=pl.ANY)] * 3 + [vm],
        out_specs=(vm, vm),
        scratch_shapes=[
            pltpu.VMEM((3, 48, 128), BF16),
            pltpu.VMEM((3, 32, 384), BF16),
            pltpu.VMEM((NCTX, KW, BLK), jnp.int32),
            pltpu.VMEM((NCTX, 1, BLK), F32),
            pltpu.VMEM((8, 48, 128), BF16),
            pltpu.VMEM((2, 4, 4, 64, 512), BF16),
            pltpu.VMEM((16, 2, 32, 384), BF16),
            pltpu.VMEM((4, 16, 2, 32, 256), BF16),
            pltpu.VMEM((384, 1024), BF16),
            pltpu.VMEM((NCTX * BLK, HD), BF16),
            pltpu.VMEM((80, NCTX * BLK), BF16),
            pltpu.VMEM((4, HD, 4 * BLK), BF16),
            pltpu.VMEM((BLK, D), BF16),
            pltpu.VMEM((4, BLK, BLK), BF16),
            pltpu.VMEM((4, BLK, BLK), BF16),
            pltpu.VMEM((128, 128), F32),
            pltpu.VMEM((NCTX, D, BLK), BF16),
            pltpu.VMEM((NCTX, 128, BLK), F32),
            pltpu.VMEM((4, BLK, BLK), F32),
            pltpu.VMEM((D, BLK), F32),
            pltpu.VMEM((HD // 2, NCTX * BLK), F32),
            pltpu.VMEM((HD // 2, NCTX * BLK), F32),
            pltpu.VMEM((BLK, D), BF16),
            pltpu.SemaphoreType.DMA((3,)),
        ]
        + [
            dma((n,))
            for n in (16, 16, 16, 16, 12, 8, 4, 4, 3, 3, 6, 6, 4, 4, 18, 17, 1, 1, 18, 17, 3, 3, 1, 1, 4, 4)
        ],
        compiler_params=pltpu.CompilerParams(
            collective_id=0, has_side_effects=True, vmem_limit_bytes=56 * 2**20
        ),
    )(byte_ids, byte_table, w_conv, w_qkv, w_out, norm_gain.reshape(8, 128), jnp.asarray(cos), jnp.asarray(sin), teacher[0], align)
    return hidden[None], loss


def solution(mesh):
    in_specs = (
        P("fsdp", "ctx"),
        P(),
        P("fsdp", None),
        P("fsdp", None),
        P("fsdp", None),
        P(),
        P("fsdp", "ctx", None),
        P("fsdp", "ctx"),
    )
    out_specs = (P("fsdp", "ctx", None), P("fsdp", "ctx"))
    return jax.shard_map(body, mesh=mesh, in_specs=in_specs, out_specs=out_specs, check_vma=False)
```

```python
import math

import jax
import jax.numpy as jnp
import numpy as np
from jax import lax
from jax.experimental import pallas as pl
from jax.experimental.pallas import tpu as pltpu
from jax.sharding import PartitionSpec as P

KW = 4
HQ = 16
HK = 4
HD = 64
D = 1024
BLK = 256
NCTX = 16
theta_base = 500000.0
norm_eps = 1e-05
masked_score = -1e30
MESH = pl.DeviceIdType.MESH
F32 = jnp.float32
BF16 = jnp.bfloat16


def rope_tables(length):
    half = HD // 2
    frequency = theta_base ** (-np.arange(half, dtype=np.float64) * 2.0 / HD)
    angles = frequency[:, None] * np.arange(length, dtype=np.float64)[None, :]
    return np.cos(angles).astype(np.float32), np.sin(angles).astype(np.float32)


def rc(src, dst, send, recv, dev):
    return pltpu.make_async_remote_copy(
        src_ref=src, dst_ref=dst, send_sem=send, recv_sem=recv, device_id=dev, device_id_type=MESH
    )


def tn(a, b):
    return lax.dot_general(a, b, (((0,), (0,)), ((), ())), preferred_element_type=F32)


def kernel(
    ids_ref, bt_ref, wconv_ref, wqkv_ref, wo_ref, gain_ref, cos_hbm, sin_hbm, teach_hbm, align_ref,
    hid_ref, loss_ref,
    wc_src, wq_src, ids_all, scale_all, wc_all, tt, wg, wo, ut, k_scr, vt_scr, qt_scr, lat_scr, att_out, att_in,
    gain_scr, hot, raw_kv, raw_q, lat_acc, cos_ref, sin_ref, teach_ref, in_s,
    ids_s, ids_r, sc_s, sc_r, wc_s, wc_r, ty_s, ty_r, t3_s, t3_r, t4_s, t4_r, t5_s, t5_r,
    wg_s, wg_r, wgx_s, wgx_r, wo_s, wo_r, wo2_s, wo2_r, wo3_s, wo3_r, at_s, at_r,
):
    f = lax.axis_index("fsdp")
    c = lax.axis_index("ctx")
    core = f % 2
    y, zh = f // 4, (f // 2) % 2
    zl, x = c // 4, c % 4
    tap = f // 8
    sib = (f // 2) * 2 + 1 - core
    zfull = zh * 4 + zl
    steps = (1, -1, 2)

    def loop(lo, hi, fn):
        def step(i, carry):
            fn(i)
            return carry

        lax.fori_loop(lo, hi, step, 0)

    def ctx_peer(i):
        return (f, (c + i) % NCTX)

    def y_peer(i):
        return (((y + i) % 8) * 4 + zh * 2 + core, c)

    def mate_row(d):
        return y - y % 2 + (y + d // 2) % 2

    def block_dev(step, d):
        z2 = (zfull + step + 8) % 8
        return (mate_row(d) * 4 + (z2 // 4) * 2 + (core + d) % 2, (z2 % 4) * 4 + x)

    def z_dev(step):
        return block_dev(step, 0)

    def x_dev(step):
        return (f, zl * 4 + (x + step + 4) % 4)

    barrier = pltpu.get_barrier_semaphore()

    def sig(dev):
        pl.semaphore_signal(barrier, inc=1, device_id=dev, device_id_type=MESH)

    for d in range(4):
        for step in (1, -1, 2, -2):
            sig(block_dev(step, d))
    for d in range(1, 4):
        sig(block_dev(0, d))
    loop(1, 8, lambda i: sig(y_peer(i)))
    loop(1, 16, lambda i: sig(ctx_peer(i)))

    reach = jnp.where(zl == 3, 1, -1)
    at_edge = (zl == 3) | (zl == 0)

    def pack_conv(slot, z):
        col = z * 4 + x
        both = wconv_ref[:, pl.ds(pl.multiple_of(col // 2 * 128, 128), 128)]
        mine = jnp.where(col % 2 == 0, both[:, :64], both[:, 64:])
        wc_src[slot] = jnp.concatenate([mine[:48], mine[48:]], axis=1)

    def mate_slot(d, half_z):
        return (y + d // 2) % 2 * 4 + half_z * 2 + (core + d) % 2

    my_slot = mate_slot(0, zh)
    pack_conv(0, zl)
    for t in (1, 2):
        pack_conv(t, (zl + reach * t + 4) % 4)
    wc_all[my_slot] = wc_src[0]
    pl.semaphore_wait(barrier, 16 + 3 + 7 + 15)

    def wc_copy(d, slot):
        return rc(wc_src.at[0], wc_all.at[slot], wc_s.at[d], wc_r.at[d], block_dev(0, d))

    def wc_near(t, d, slot):
        return rc(
            wc_src.at[t], wc_all.at[slot], wc_s.at[4 * t + d], wc_r.at[4 + d], block_dev(reach * t, d)
        )

    @pl.when(at_edge)
    def _():
        for t in (1, 2):
            for d in range(4):
                wc_near(t, d, my_slot).start()

    for d in range(1, 4):
        wc_copy(d, my_slot).start()

    late = [
        pltpu.make_async_copy(src, dst, in_s.at[n])
        for n, (src, dst) in enumerate(((cos_hbm, cos_ref), (sin_hbm, sin_ref), (teach_hbm, teach_ref)))
    ]
    for copy in late:
        copy.start()

    taps = lax.broadcasted_iota(jnp.int32, (8, 4 * BLK), 0)
    at = lax.broadcasted_iota(jnp.int32, (8, 4 * BLK), 1)
    spread = jnp.where(at % KW == taps, jnp.broadcast_to(ids_ref[...], (8, 4 * BLK)).astype(F32), 0.0)
    to_row = lax.broadcasted_iota(jnp.int32, (4 * BLK, BLK), 0) // KW
    to_row = (to_row == lax.broadcasted_iota(jnp.int32, (4 * BLK, BLK), 1)).astype(BF16)
    rows_of = jnp.dot(spread.astype(BF16), to_row, preferred_element_type=F32)
    ids_all[c] = rows_of[:KW].astype(jnp.int32)

    def ids_copy(i, slot):
        ref = ids_all.at[slot]
        return rc(ref, ref, ids_s.at[i], ids_r.at[i], ctx_peer(i))

    gains = gain_ref[...].astype(F32)
    here = lax.broadcasted_iota(jnp.int32, (8, 128), 0) == f // 4
    gains = jnp.sum(jnp.where(here, gains, 0.0), axis=0, keepdims=True)
    gain_scr[...] = jnp.broadcast_to(gains, (128, 128)).T
    my_gain = gain_scr[pl.ds(pl.multiple_of(f % 4 * 32, 32), 32), 0:1]

    def pack_heads(slot, z):
        def heads_of(start):
            two = wqkv_ref[:, pl.ds(pl.multiple_of(start + z // 2 * 128, 128), 128)]
            return jnp.where(z % 2 == 0, two[:, :64], two[:, 64:])

        mine = jnp.concatenate(
            [wqkv_ref[:, pl.ds(pl.multiple_of(z * 256, 256), 256)], heads_of(HQ * HD), heads_of((HQ + HK) * HD)],
            axis=1,
        )
        wq_src[slot] = (mine.astype(F32) * my_gain).astype(BF16)

    pack_heads(0, zl)
    for t in (1, 2):
        pack_heads(t, (zl + reach * t + 4) % 4)
    wg[y * 2 + zh, core] = wq_src[0]

    def quarter(z):
        return jnp.where(core == 0, x, z)

    def wo_cols(z):
        return wo_ref.at[:, pl.ds(pl.multiple_of(quarter(z) * 256, 256), 256)]

    my_quarter = quarter(zl)
    wo[my_quarter, y * 2 + zh, core] = wo_ref[:, pl.ds(pl.multiple_of(my_quarter * 256, 256), 256)]

    def wq_near(t, slot):
        return rc(wq_src.at[t], wg.at[slot, core], wg_s.at[15 + t], wg_r.at[16], z_dev(reach * t))

    def wo_near(t, slot):
        z = (zl + reach * t + 4) % 4
        return rc(wo_cols(z), wo.at[quarter(z), slot, core], wo_s.at[15 + t], wo_r.at[16], z_dev(reach * t))

    @pl.when(at_edge)
    def _():
        for t in (1, 2):
            wq_near(t, y * 2 + zh).start()
            wo_near(t, y * 2 + zh).start()

    loop(1, 16, lambda i: ids_copy(i, c).start())

    def wg_copy(i, row, half_z):
        ref = wg.at[row * 2 + half_z, core]
        n = i + 8 * jnp.where(half_z == zh, 0, 1)
        return rc(ref, ref, wg_s.at[n], wg_r.at[n], y_peer(i))

    def wo_copy(i, row, half_z):
        ref = wo.at[my_quarter, row * 2 + half_z, core]
        n = i + 8 * jnp.where(half_z == zh, 0, 1)
        return rc(ref, ref, wo_s.at[n], wo_r.at[n], y_peer(i))

    loop(1, 8, lambda i: wg_copy(i, y, zh).start())

    btt = bt_ref[...].T
    bta = jnp.concatenate([btt[m * 96 : m * 96 + 48] for m in range(8)], axis=0)
    btb = jnp.concatenate([btt[m * 96 + 48 : m * 96 + 96] for m in range(8)], axis=0)

    for d in range(1, 4):
        wc_copy(d, mate_slot(d, zh)).wait_recv()
    for d in range(4):
        wc_near(1, d, mate_slot(d, 1 - zh)).wait_recv()
    wc_val = wc_all[...].reshape(384, 128)
    piece = tn(wc_val, bta)[:64] + tn(wc_val, btb)[64:]

    away = jnp.where(y % 2 == 0, -1, 1)

    def y_copy(step, from_tap):
        ref = tt.at[core, zl, x, :, pl.ds(pl.multiple_of(from_tap % 2 * 256, 256), 256)]
        return rc(ref, ref, ty_s.at[step], ty_r.at[step], y_peer(8 + away * step))

    @pl.when(tap // 2 == core)
    def _():
        tt[core, zl, x, :, pl.ds(pl.multiple_of(tap % 2 * 256, 256), 256)] = piece.astype(BF16)
        for step in (1, 2, 3):
            y_copy(step, tap).start()

    wq_near(1, y * 2 + 1 - zh).wait_recv()
    loop(1, 8, lambda i: wg_copy(i, y, 1 - zh).start())

    for step in (1, 2, 3):
        src_tap = (tap + (away, -away, 2)[step - 1] + 4) % 4

        @pl.when(src_tap // 2 == core)
        def _():
            y_copy(step, src_tap).wait_recv()

    own = tt.at[core, zl, x]

    def first_copy(n, dev, ref):
        return rc(ref, ref, t3_s.at[n], t3_r.at[n], dev)

    ways = (1, -1, 1, -1, 1, -1)
    parts = (0, 2, 2, 0, 0, 2)

    def along_x(n, shift):
        ref = tt.at[core, pl.ds(parts[n], 2), (x + shift + 4) % 4]
        return rc(ref, ref, t4_s.at[n], t4_r.at[n], x_dev(ways[n]))

    def along_z(n, shift):
        ref = tt.at[core, (zl + shift + 4) % 4, pl.ds(parts[n], 2)]
        return rc(ref, ref, t4_s.at[n], t4_r.at[n], z_dev(ways[n]))

    def make_hot(b, carry):
        rows = lax.broadcasted_iota(jnp.int32, (256, BLK), 0)
        block = ids_all[b]
        for k in range(KW):
            hot[b, k * 256 : (k + 1) * 256] = (block[k : k + 1, :] == rows).astype(BF16)
        return carry

    def meanwhile():
        loop(1, 8, lambda i: wo_copy(i, y, zh).start())
        rc(
            wo_cols(zl), wo.at[my_quarter, y * 2 + 1 - zh, core], wo_s.at[16], wo_r.at[16], z_dev(1)
        ).wait_recv()
        loop(1, 8, lambda i: wo_copy(i, y, 1 - zh).start())

        loop(1, 16, lambda i: ids_copy(i, (c - i + NCTX) % NCTX).wait_recv())
        lax.fori_loop(0, NCTX, make_hot, 0)
        for d in range(1, 4):
            wc_copy(d, my_slot).wait_send()

        @pl.when(at_edge)
        def _():
            for t in (1, 2):
                for d in range(4):
                    wc_near(t, d, my_slot).wait_send()

        loop(1, 16, lambda i: ids_copy(i, c).wait_send())

        @pl.when(tap // 2 == core)
        def _():
            for step in (1, 2, 3):
                y_copy(step, tap).wait_send()

        for n, s in enumerate(steps):
            first_copy(n, z_dev(s), own).wait_send()

    def over(n, ref):
        return rc(ref, ref, t5_s.at[n], t5_r.at[n], (sib, c))

    def second_axis(along, slice_of):
        over(0, slice_of(0, core)).start()
        along(0, -1).wait_recv()
        along(4, -1).start()
        along(1, 1).wait_recv()
        along(5, 1).start()
        meanwhile()
        along(2, -1).wait_recv()
        over(1, slice_of(-1, core)).start()
        along(3, 1).wait_recv()
        over(2, slice_of(1, core)).start()
        along(4, -2).wait_recv()
        along(5, 2).wait_recv()
        over(3, slice_of(2, core)).start()

    def slice_x(shift, part):
        return tt.at[part, :, (x + shift + 4) % 4]

    def slice_z(shift, part):
        return tt.at[part, (zl + shift + 4) % 4]

    @pl.when(core == 0)
    def _():
        for n, s in enumerate(steps):
            first_copy(n, z_dev(s), own).start()
        for n, s in enumerate(steps):
            first_copy(n, z_dev(s), tt.at[core, (zl - s + 4) % 4, x]).wait_recv()
        for n in (0, 1, 2, 3):
            along_x(n, 0).start()

    @pl.when(core == 1)
    def _():
        for n, s in enumerate(steps):
            first_copy(n, x_dev(s), own).start()
        for n, s in enumerate(steps):
            first_copy(n, x_dev(s), tt.at[core, zl, (x - s + 4) % 4]).wait_recv()
        for n in (0, 1, 2, 3):
            along_z(n, 0).start()

    @pl.when(core == 0)
    def _():
        second_axis(along_x, slice_x)

    @pl.when(core == 1)
    def _():
        second_axis(along_z, slice_z)

    for half_z in (0, 1):
        loop(1, 8, lambda i: wg_copy(i, (y - i + 8) % 8, half_z).wait_recv())
    rc(wg.at[:, core], wg.at[:, core], wgx_s.at[0], wgx_r.at[0], (sib, c)).start()

    def table(part):
        return tt[part].reshape(D, 512)

    def hot_rows(b, part):
        return hot[b, pl.ds(pl.multiple_of(part * 512, 512), 512)]

    lat_acc[...] = jnp.dot(table(core), hot_rows(c, core), preferred_element_type=F32)

    @pl.when(core == 0)
    def _():
        for n, shift in enumerate((0, -1, 1, 2)):
            over(n, slice_z(shift, 1 - core)).wait_recv()

    @pl.when(core == 1)
    def _():
        for n, shift in enumerate((0, -1, 1, 2)):
            over(n, slice_x(shift, 1 - core)).wait_recv()

    latent = lat_acc[...] + jnp.dot(table(1 - core), hot_rows(c, 1 - core), preferred_element_type=F32)
    latent = latent.astype(BF16)
    wide = latent.astype(F32)
    scale = lax.rsqrt(jnp.sum(wide * wide, axis=0, keepdims=True) * (1.0 / D) + norm_eps)
    scale_all[c] = scale

    def sc_copy(i, slot):
        ref = scale_all.at[slot]
        return rc(ref, ref, sc_s.at[i], sc_r.at[i], ctx_peer(i))

    loop(1, 16, lambda i: sc_copy(i, c).start())
    lat_scr[...] = latent.T

    ref = wg.at[:, 1 - core]
    rc(ref, ref, wgx_s.at[0], wgx_r.at[0], (sib, c)).wait_recv()
    wgt = wg[...].reshape(D, 384)
    for part in (0, 1):
        ut[:, part * 512 : (part + 1) * 512] = tn(wgt, table(part)).astype(BF16)

    def make_kv(b, carry):
        raw_kv[b] = jnp.dot(ut[256:384, :], hot[b], preferred_element_type=F32)
        return carry

    def make_q(zb, carry):
        raw_q[zb] = jnp.dot(ut[:256, :], hot[zb * 4 + x], preferred_element_type=F32)
        return carry

    lax.fori_loop(0, NCTX, make_kv, 0)
    lax.fori_loop(0, 4, make_q, 0)

    for half_z in (0, 1):
        loop(1, 8, lambda i: wo_copy(i, (y - i + 8) % 8, half_z).wait_recv())

    def wo2_copy(n, dev, slot):
        ref = wo.at[slot, :, core]
        return rc(ref, ref, wo2_s.at[n], wo2_r.at[n], dev)

    @pl.when(core == 0)
    def _():
        for n, s in enumerate(steps):
            wo2_copy(n, x_dev(s), my_quarter).start()

    @pl.when(core == 1)
    def _():
        for n, s in enumerate(steps):
            wo2_copy(n, z_dev(s), my_quarter).start()

    loop(1, 16, lambda i: sc_copy(i, (c - i + NCTX) % NCTX).wait_recv())

    def turn(v, b, scale_row):
        cols = pl.ds(pl.multiple_of(b * BLK, BLK), BLK)
        cos, sin = cos_ref[:, cols] * scale_row, sin_ref[:, cols] * scale_row
        lo, hi = v[:32], v[32:]
        return jnp.concatenate([lo * cos - hi * sin, hi * cos + lo * sin], axis=0)

    def turn_kv(b, carry):
        cols = pl.ds(pl.multiple_of(b * BLK, BLK), BLK)
        k_scr[pl.ds(pl.multiple_of(b * BLK, BLK), BLK), :] = (
            turn(raw_kv[b, :64], b, scale_all[b]).astype(BF16).T
        )
        vt_scr[:64, cols] = (raw_kv[b, 64:] * scale_all[b]).astype(BF16)
        return carry

    def turn_q(zb, carry):
        b = zb * 4 + x
        row = scale_all[b] * (math.log2(math.e) / math.sqrt(HD))
        for h in range(4):
            qt_scr[zb, :, h * BLK : (h + 1) * BLK] = turn(raw_q[zb, h * HD : (h + 1) * HD], b, row).astype(BF16)
        return carry

    vt_scr[64:, :] = jnp.ones_like(vt_scr[64:, :])
    for copy in late:
        copy.wait()
    lax.fori_loop(0, NCTX, turn_kv, 0)
    lax.fori_loop(0, 4, turn_q, 0)

    def scores(zb, i, h):
        keys = k_scr[pl.ds(pl.multiple_of(i * BLK, BLK), BLK), :]
        return jnp.dot(keys, qt_scr[zb, :, h * BLK : (h + 1) * BLK], preferred_element_type=F32)

    def soft(i, s, state):
        top, acc = state
        new_top = jnp.maximum(top, jnp.max(s, axis=0, keepdims=True))
        probs = jnp.exp2(s - new_top).astype(BF16)
        values = vt_scr[:, pl.ds(pl.multiple_of(i * BLK, BLK), BLK)]
        acc = acc * jnp.exp2(top - new_top) + jnp.dot(values, probs, preferred_element_type=F32)
        return new_top, acc

    key_row = lax.broadcasted_iota(jnp.int32, (BLK, BLK), 0)
    query_row = lax.broadcasted_iota(jnp.int32, (BLK, BLK), 1) + x * BLK

    def attend(zb):
        def one(i, carry, masked_block):
            states, now = carry
            later, new_states = [], []
            for h in range(4):
                if masked_block != 3:
                    later.append(scores(zb, i + 1, h))
                s = now[h]
                if masked_block is not None:
                    s = jnp.where(key_row + masked_block * BLK <= query_row, s, masked_score)
                new_states.append(soft(i, s, states[h]))
            return new_states, later

        def four(j, carry):
            for k in range(4):
                carry = one(j * 4 + k, carry, None)
            return carry

        carry = (
            [(jnp.full((1, BLK), masked_score, F32), jnp.zeros((80, BLK), F32)) for _ in range(4)],
            [scores(zb, 0, h) for h in range(4)],
        )
        for j in range(zb):
            carry = four(j, carry)
        for k in range(4):
            carry = one(4 * zb + k, carry, k)
        for h in range(4):
            _, acc = carry[0][h]
            att_out[zb, h * HD : (h + 1) * HD] = (acc[:HD] / acc[HD : HD + 1]).astype(BF16)

    def att_copy(zb, slot):
        return rc(att_out.at[zb], att_in.at[slot], at_s.at[zb], at_r.at[slot], (f, zb * 4 + x))

    def block_step(i, carry):
        zb = (zl + i) % 4

        @pl.when(i == 3)
        def _():
            for n, s in enumerate(steps):
                wo2_copy(n, x_dev(s), (my_quarter - s + 4) % 4).wait_recv()
            rc(wo.at[:, :, core], wo.at[:, :, core], wo3_s.at[0], wo3_r.at[0], (sib, c)).start()

        for k in range(4):

            @pl.when(zb == k)
            def _():
                attend(k)

        @pl.when(i < 4)
        def _():
            att_copy(zb, zl).start()

        return carry

    lax.fori_loop(1, 5, block_step, 0)
    att_in[zl] = att_out[zl]

    @pl.when(at_edge)
    def _():
        for t in (1, 2):
            wq_near(t, y * 2 + zh).wait_send()
            wo_near(t, y * 2 + zh).wait_send()

    loop(1, 16, lambda i: sc_copy(i, c).wait_send())
    for half_z in (0, 1):
        loop(1, 8, lambda i: wg_copy(i, y, half_z).wait_send())
        loop(1, 8, lambda i: wo_copy(i, y, half_z).wait_send())

    for n, s in enumerate(steps):
        wo2_copy(n, x_dev(s), my_quarter).wait_send()
    for n in range(6):
        along_x(n, 0).wait_send()
    for n in range(4):
        over(n, slice_x(0, core)).wait_send()
    rc(wg.at[:, core], wg.at[:, core], wgx_s.at[0], wgx_r.at[0], (sib, c)).wait_send()

    ref = wo.at[:, :, 1 - core]
    rc(ref, ref, wo3_s.at[0], wo3_r.at[0], (sib, c)).wait_recv()
    for i in (1, 2, 3):
        slot = (zl - i + 4) % 4
        att_copy(slot, slot).wait_recv()

    attended = att_in[...].reshape(D, BLK).T
    pick = (align_ref[...] - c * BLK == lax.broadcasted_iota(jnp.int32, (BLK, BLK), 0)).astype(BF16)
    total = jnp.zeros((BLK, 1), F32)
    for j in range(4):
        cols = pl.ds(j * 256, 256)
        branch = jnp.dot(attended, wo[j].reshape(D, 256), preferred_element_type=F32)
        hidden = (lat_scr[:, cols].astype(F32) + branch).astype(BF16)
        hid_ref[:, cols] = hidden
        diff = tn(pick, hidden) - teach_ref[:, cols].astype(F32)
        total = total + jnp.sum(diff * diff, axis=1, keepdims=True)
    loss_ref[...] = jnp.broadcast_to(total * (1.0 / D), (BLK, 128)).T[0:1, :]

    rc(wo.at[:, :, core], wo.at[:, :, core], wo3_s.at[0], wo3_r.at[0], (sib, c)).wait_send()
    for i in (1, 2, 3):
        att_copy((zl + i) % 4, zl).wait_send()


def body(byte_ids, byte_table, w_conv, w_qkv, w_out, norm_gain, teacher, align):
    cos, sin = rope_tables(NCTX * BLK)
    vm = pl.BlockSpec(memory_space=pltpu.VMEM)
    dma = pltpu.SemaphoreType.DMA
    hidden, loss = pl.pallas_call(
        kernel,
        out_shape=(
            jax.ShapeDtypeStruct((BLK, D), BF16),
            jax.ShapeDtypeStruct((1, BLK), F32),
        ),
        in_specs=[vm] * 6 + [pl.BlockSpec(memory_space=pl.ANY)] * 3 + [vm],
        out_specs=(vm, vm),
        scratch_shapes=[
            pltpu.VMEM((3, 48, 128), BF16),
            pltpu.VMEM((3, 32, 384), BF16),
            pltpu.VMEM((NCTX, KW, BLK), jnp.int32),
            pltpu.VMEM((NCTX, 1, BLK), F32),
            pltpu.VMEM((8, 48, 128), BF16),
            pltpu.VMEM((2, 4, 4, 64, 512), BF16),
            pltpu.VMEM((16, 2, 32, 384), BF16),
            pltpu.VMEM((4, 16, 2, 32, 256), BF16),
            pltpu.VMEM((384, 1024), BF16),
            pltpu.VMEM((NCTX * BLK, HD), BF16),
            pltpu.VMEM((80, NCTX * BLK), BF16),
            pltpu.VMEM((4, HD, 4 * BLK), BF16),
            pltpu.VMEM((BLK, D), BF16),
            pltpu.VMEM((4, BLK, BLK), BF16),
            pltpu.VMEM((4, BLK, BLK), BF16),
            pltpu.VMEM((128, 128), F32),
            pltpu.VMEM((NCTX, D, BLK), BF16),
            pltpu.VMEM((NCTX, 128, BLK), F32),
            pltpu.VMEM((4, BLK, BLK), F32),
            pltpu.VMEM((D, BLK), F32),
            pltpu.VMEM((HD // 2, NCTX * BLK), F32),
            pltpu.VMEM((HD // 2, NCTX * BLK), F32),
            pltpu.VMEM((BLK, D), BF16),
            pltpu.SemaphoreType.DMA((3,)),
        ]
        + [
            dma((n,))
            for n in (16, 16, 16, 16, 12, 8, 4, 4, 3, 3, 6, 6, 4, 4, 18, 17, 1, 1, 18, 17, 3, 3, 1, 1, 4, 4)
        ],
        compiler_params=pltpu.CompilerParams(
            collective_id=0, has_side_effects=True, vmem_limit_bytes=56 * 2**20
        ),
    )(byte_ids, byte_table, w_conv, w_qkv, w_out, norm_gain.reshape(8, 128), jnp.asarray(cos), jnp.asarray(sin), teacher[0], align)
    return hidden[None], loss


def solution(mesh):
    in_specs = (
        P("fsdp", "ctx"),
        P(),
        P("fsdp", None),
        P("fsdp", None),
        P("fsdp", None),
        P(),
        P("fsdp", "ctx", None),
        P("fsdp", "ctx"),
    )
    out_specs = (P("fsdp", "ctx", None), P("fsdp", "ctx"))
    return jax.shard_map(body, mesh=mesh, in_specs=in_specs, out_specs=out_specs, check_vma=False)
```

```python
import math

import jax
import jax.numpy as jnp
import numpy as np
from jax import lax
from jax.experimental import pallas as pl
from jax.experimental.pallas import tpu as pltpu
from jax.sharding import PartitionSpec as P

KW = 4
HQ = 16
HK = 4
HD = 64
D = 1024
BLK = 256
NCTX = 16
theta_base = 500000.0
norm_eps = 1e-05
masked_score = -1e30
MESH = pl.DeviceIdType.MESH
F32 = jnp.float32
BF16 = jnp.bfloat16


def rope_tables(length):
    half = HD // 2
    frequency = theta_base ** (-np.arange(half, dtype=np.float64) * 2.0 / HD)
    angles = frequency[:, None] * np.arange(length, dtype=np.float64)[None, :]
    return np.cos(angles).astype(np.float32), np.sin(angles).astype(np.float32)


def rc(src, dst, send, recv, dev):
    return pltpu.make_async_remote_copy(
        src_ref=src, dst_ref=dst, send_sem=send, recv_sem=recv, device_id=dev, device_id_type=MESH
    )


def tn(a, b):
    return lax.dot_general(a, b, (((0,), (0,)), ((), ())), preferred_element_type=F32)


def kernel(
    ids_ref, bt_ref, wconv_ref, wqkv_ref, wo_ref, gain_ref, cos_hbm, sin_hbm, teach_hbm, align_ref,
    hid_ref, loss_ref,
    wc_src, wq_src, ids_all, scale_all, wc_all, tt, wg, wo, ut, k_scr, vt_scr, qt_scr, lat_scr, att_out, att_in,
    gain_scr, hot, raw_kv, raw_q, lat_acc, cos_ref, sin_ref, teach_ref, in_s,
    ids_s, ids_r, sc_s, sc_r, wc_s, wc_r, ty_s, ty_r, t3_s, t3_r, t4_s, t4_r, t5_s, t5_r,
    wg_s, wg_r, wgx_s, wgx_r, wo_s, wo_r, wo2_s, wo2_r, wo3_s, wo3_r, at_s, at_r,
):
    f = lax.axis_index("fsdp")
    c = lax.axis_index("ctx")
    core = f % 2
    y, zh = f // 4, (f // 2) % 2
    zl, x = c // 4, c % 4
    tap = f // 8
    sib = (f // 2) * 2 + 1 - core
    zfull = zh * 4 + zl
    steps = (1, -1, 2)

    def loop(lo, hi, fn):
        def step(i, carry):
            fn(i)
            return carry

        lax.fori_loop(lo, hi, step, 0)

    def ctx_peer(i):
        return (f, (c + i) % NCTX)

    def y_peer(i):
        return (((y + i) % 8) * 4 + zh * 2 + core, c)

    def mate_row(d):
        return y - y % 2 + (y + d // 2) % 2

    def block_dev(step, d):
        z2 = (zfull + step + 8) % 8
        return (mate_row(d) * 4 + (z2 // 4) * 2 + (core + d) % 2, (z2 % 4) * 4 + x)

    def z_dev(step):
        return block_dev(step, 0)

    def x_dev(step):
        return (f, zl * 4 + (x + step + 4) % 4)

    barrier = pltpu.get_barrier_semaphore()

    def sig(dev):
        pl.semaphore_signal(barrier, inc=1, device_id=dev, device_id_type=MESH)

    for d in range(4):
        for step in (1, -1, 2, -2):
            sig(block_dev(step, d))
    for d in range(1, 4):
        sig(block_dev(0, d))
    loop(1, 8, lambda i: sig(y_peer(i)))
    loop(1, 16, lambda i: sig(ctx_peer(i)))

    reach = jnp.where(zl == 3, 1, -1)
    at_edge = (zl == 3) | (zl == 0)

    def pack_conv(slot, z):
        col = z * 4 + x
        both = wconv_ref[:, pl.ds(pl.multiple_of(col // 2 * 128, 128), 128)]
        mine = jnp.where(col % 2 == 0, both[:, :64], both[:, 64:])
        wc_src[slot] = jnp.concatenate([mine[:48], mine[48:]], axis=1)

    def mate_slot(d, half_z):
        return (y + d // 2) % 2 * 4 + half_z * 2 + (core + d) % 2

    my_slot = mate_slot(0, zh)
    pack_conv(0, zl)
    for t in (1, 2):
        pack_conv(t, (zl + reach * t + 4) % 4)
    wc_all[my_slot] = wc_src[0]
    pl.semaphore_wait(barrier, 16 + 3 + 7 + 15)

    def wc_copy(d, slot):
        return rc(wc_src.at[0], wc_all.at[slot], wc_s.at[d], wc_r.at[d], block_dev(0, d))

    def wc_near(t, d, slot):
        return rc(
            wc_src.at[t], wc_all.at[slot], wc_s.at[4 * t + d], wc_r.at[4 + d], block_dev(reach * t, d)
        )

    @pl.when(at_edge)
    def _():
        for t in (1, 2):
            for d in range(4):
                wc_near(t, d, my_slot).start()

    for d in range(1, 4):
        wc_copy(d, my_slot).start()

    late = [
        pltpu.make_async_copy(src, dst, in_s.at[n])
        for n, (src, dst) in enumerate(((cos_hbm, cos_ref), (sin_hbm, sin_ref), (teach_hbm, teach_ref)))
    ]
    for copy in late:
        copy.start()

    taps = lax.broadcasted_iota(jnp.int32, (8, 4 * BLK), 0)
    at = lax.broadcasted_iota(jnp.int32, (8, 4 * BLK), 1)
    spread = jnp.where(at % KW == taps, jnp.broadcast_to(ids_ref[...], (8, 4 * BLK)).astype(F32), 0.0)
    to_row = lax.broadcasted_iota(jnp.int32, (4 * BLK, BLK), 0) // KW
    to_row = (to_row == lax.broadcasted_iota(jnp.int32, (4 * BLK, BLK), 1)).astype(BF16)
    rows_of = jnp.dot(spread.astype(BF16), to_row, preferred_element_type=F32)
    ids_all[c] = rows_of[:KW].astype(jnp.int32)

    def ids_copy(i, slot):
        ref = ids_all.at[slot]
        return rc(ref, ref, ids_s.at[i], ids_r.at[i], ctx_peer(i))

    gains = gain_ref[...].astype(F32)
    here = lax.broadcasted_iota(jnp.int32, (8, 128), 0) == f // 4
    gains = jnp.sum(jnp.where(here, gains, 0.0), axis=0, keepdims=True)
    gain_scr[...] = jnp.broadcast_to(gains, (128, 128)).T
    my_gain = gain_scr[pl.ds(pl.multiple_of(f % 4 * 32, 32), 32), 0:1]

    def pack_heads(slot, z):
        def heads_of(start):
            two = wqkv_ref[:, pl.ds(pl.multiple_of(start + z // 2 * 128, 128), 128)]
            return jnp.where(z % 2 == 0, two[:, :64], two[:, 64:])

        mine = jnp.concatenate(
            [wqkv_ref[:, pl.ds(pl.multiple_of(z * 256, 256), 256)], heads_of(HQ * HD), heads_of((HQ + HK) * HD)],
            axis=1,
        )
        wq_src[slot] = (mine.astype(F32) * my_gain).astype(BF16)

    pack_heads(0, zl)
    for t in (1, 2):
        pack_heads(t, (zl + reach * t + 4) % 4)
    wg[y * 2 + zh, core] = wq_src[0]

    def quarter(z):
        return jnp.where(core == 0, x, z)

    def wo_cols(z):
        return wo_ref.at[:, pl.ds(pl.multiple_of(quarter(z) * 256, 256), 256)]

    my_quarter = quarter(zl)
    wo[my_quarter, y * 2 + zh, core] = wo_ref[:, pl.ds(pl.multiple_of(my_quarter * 256, 256), 256)]

    def wq_near(t, slot):
        return rc(wq_src.at[t], wg.at[slot, core], wg_s.at[15 + t], wg_r.at[16], z_dev(reach * t))

    def wo_near(t, slot):
        z = (zl + reach * t + 4) % 4
        return rc(wo_cols(z), wo.at[quarter(z), slot, core], wo_s.at[15 + t], wo_r.at[16], z_dev(reach * t))

    @pl.when(at_edge)
    def _():
        for t in (1, 2):
            wq_near(t, y * 2 + zh).start()
            wo_near(t, y * 2 + zh).start()

    loop(1, 16, lambda i: ids_copy(i, c).start())

    def wg_copy(i, row, half_z):
        ref = wg.at[row * 2 + half_z, core]
        n = i + 8 * jnp.where(half_z == zh, 0, 1)
        return rc(ref, ref, wg_s.at[n], wg_r.at[n], y_peer(i))

    def wo_copy(i, row, half_z):
        ref = wo.at[my_quarter, row * 2 + half_z, core]
        n = i + 8 * jnp.where(half_z == zh, 0, 1)
        return rc(ref, ref, wo_s.at[n], wo_r.at[n], y_peer(i))

    loop(1, 8, lambda i: wg_copy(i, y, zh).start())

    btt = bt_ref[...].T
    bta = jnp.concatenate([btt[m * 96 : m * 96 + 48] for m in range(8)], axis=0)
    btb = jnp.concatenate([btt[m * 96 + 48 : m * 96 + 96] for m in range(8)], axis=0)

    for d in range(1, 4):
        wc_copy(d, mate_slot(d, zh)).wait_recv()
    for d in range(4):
        wc_near(1, d, mate_slot(d, 1 - zh)).wait_recv()
    wc_val = wc_all[...].reshape(384, 128)
    piece = tn(wc_val, bta)[:64] + tn(wc_val, btb)[64:]

    away = jnp.where(y % 2 == 0, -1, 1)

    def y_copy(step, from_tap):
        ref = tt.at[core, zl, x, :, pl.ds(pl.multiple_of(from_tap % 2 * 256, 256), 256)]
        return rc(ref, ref, ty_s.at[step], ty_r.at[step], y_peer(8 + away * step))

    @pl.when(tap // 2 == core)
    def _():
        tt[core, zl, x, :, pl.ds(pl.multiple_of(tap % 2 * 256, 256), 256)] = piece.astype(BF16)
        for step in (1, 2, 3):
            y_copy(step, tap).start()

    wq_near(1, y * 2 + 1 - zh).wait_recv()
    loop(1, 8, lambda i: wg_copy(i, y, 1 - zh).start())

    for step in (1, 2, 3):
        src_tap = (tap + (away, -away, 2)[step - 1] + 4) % 4

        @pl.when(src_tap // 2 == core)
        def _():
            y_copy(step, src_tap).wait_recv()

    own = tt.at[core, zl, x]

    def first_copy(n, dev, ref):
        return rc(ref, ref, t3_s.at[n], t3_r.at[n], dev)

    ways = (1, -1, 1, -1, 1, -1)
    parts = (0, 2, 2, 0, 0, 2)

    def along_x(n, shift):
        ref = tt.at[core, pl.ds(parts[n], 2), (x + shift + 4) % 4]
        return rc(ref, ref, t4_s.at[n], t4_r.at[n], x_dev(ways[n]))

    def along_z(n, shift):
        ref = tt.at[core, (zl + shift + 4) % 4, pl.ds(parts[n], 2)]
        return rc(ref, ref, t4_s.at[n], t4_r.at[n], z_dev(ways[n]))

    def make_hot(b, carry):
        rows = lax.broadcasted_iota(jnp.int32, (256, BLK), 0)
        block = ids_all[b]
        for k in range(KW):
            hot[b, k * 256 : (k + 1) * 256] = (block[k : k + 1, :] == rows).astype(BF16)
        return carry

    def meanwhile():
        rc(
            wo_cols(zl), wo.at[my_quarter, y * 2 + 1 - zh, core], wo_s.at[16], wo_r.at[16], z_dev(1)
        ).wait_recv()
        loop(1, 8, lambda i: wo_copy(i, y, 1 - zh).start())

        loop(1, 16, lambda i: ids_copy(i, (c - i + NCTX) % NCTX).wait_recv())
        lax.fori_loop(0, NCTX, make_hot, 0)
        for d in range(1, 4):
            wc_copy(d, my_slot).wait_send()

        @pl.when(at_edge)
        def _():
            for t in (1, 2):
                for d in range(4):
                    wc_near(t, d, my_slot).wait_send()

        loop(1, 16, lambda i: ids_copy(i, c).wait_send())

        @pl.when(tap // 2 == core)
        def _():
            for step in (1, 2, 3):
                y_copy(step, tap).wait_send()

        for n, s in enumerate(steps):
            first_copy(n, z_dev(s), own).wait_send()

    def over(n, ref):
        return rc(ref, ref, t5_s.at[n], t5_r.at[n], (sib, c))

    def second_axis(along, slice_of):
        over(0, slice_of(0, core)).start()
        along(0, -1).wait_recv()
        along(4, -1).start()
        along(1, 1).wait_recv()
        along(5, 1).start()
        meanwhile()
        along(2, -1).wait_recv()
        over(1, slice_of(-1, core)).start()
        along(3, 1).wait_recv()
        over(2, slice_of(1, core)).start()
        along(4, -2).wait_recv()
        along(5, 2).wait_recv()
        over(3, slice_of(2, core)).start()

    def slice_x(shift, part):
        return tt.at[part, :, (x + shift + 4) % 4]

    def slice_z(shift, part):
        return tt.at[part, (zl + shift + 4) % 4]

    @pl.when(core == 0)
    def _():
        for n, s in enumerate(steps):
            first_copy(n, z_dev(s), own).start()
        loop(1, 8, lambda i: wo_copy(i, y, zh).start())
        for n, s in enumerate(steps):
            first_copy(n, z_dev(s), tt.at[core, (zl - s + 4) % 4, x]).wait_recv()
        for n in (0, 1, 2, 3):
            along_x(n, 0).start()

    @pl.when(core == 1)
    def _():
        for n, s in enumerate(steps):
            first_copy(n, x_dev(s), own).start()
        loop(1, 8, lambda i: wo_copy(i, y, zh).start())
        for n, s in enumerate(steps):
            first_copy(n, x_dev(s), tt.at[core, zl, (x - s + 4) % 4]).wait_recv()
        for n in (0, 1, 2, 3):
            along_z(n, 0).start()

    @pl.when(core == 0)
    def _():
        second_axis(along_x, slice_x)

    @pl.when(core == 1)
    def _():
        second_axis(along_z, slice_z)

    for half_z in (0, 1):
        loop(1, 8, lambda i: wg_copy(i, (y - i + 8) % 8, half_z).wait_recv())
    rc(wg.at[:, core], wg.at[:, core], wgx_s.at[0], wgx_r.at[0], (sib, c)).start()

    def table(part):
        return tt[part].reshape(D, 512)

    def hot_rows(b, part):
        return hot[b, pl.ds(pl.multiple_of(part * 512, 512), 512)]

    lat_acc[...] = jnp.dot(table(core), hot_rows(c, core), preferred_element_type=F32)

    @pl.when(core == 0)
    def _():
        for n, shift in enumerate((0, -1, 1, 2)):
            over(n, slice_z(shift, 1 - core)).wait_recv()

    @pl.when(core == 1)
    def _():
        for n, shift in enumerate((0, -1, 1, 2)):
            over(n, slice_x(shift, 1 - core)).wait_recv()

    latent = lat_acc[...] + jnp.dot(table(1 - core), hot_rows(c, 1 - core), preferred_element_type=F32)
    latent = latent.astype(BF16)
    wide = latent.astype(F32)
    scale = lax.rsqrt(jnp.sum(wide * wide, axis=0, keepdims=True) * (1.0 / D) + norm_eps)
    scale_all[c] = scale

    def sc_copy(i, slot):
        ref = scale_all.at[slot]
        return rc(ref, ref, sc_s.at[i], sc_r.at[i], ctx_peer(i))

    loop(1, 16, lambda i: sc_copy(i, c).start())
    lat_scr[...] = latent.T

    ref = wg.at[:, 1 - core]
    rc(ref, ref, wgx_s.at[0], wgx_r.at[0], (sib, c)).wait_recv()
    wgt = wg[...].reshape(D, 384)
    for part in (0, 1):
        ut[:, part * 512 : (part + 1) * 512] = tn(wgt, table(part)).astype(BF16)

    for half_z in (0, 1):
        loop(1, 8, lambda i: wo_copy(i, (y - i + 8) % 8, half_z).wait_recv())
    far_steps = ((1, 0, 16), (-1, 0, 16), (2, 0, 8), (-2, 8, 8))

    def wo2_copy(n, dev, slot):
        ref = wo.at[slot, pl.ds(far_steps[n][1], far_steps[n][2]), core]
        return rc(ref, ref, wo2_s.at[n], wo2_r.at[n], dev)

    @pl.when(core == 0)
    def _():
        for n, s in enumerate(far_steps):
            wo2_copy(n, x_dev(s[0]), my_quarter).start()

    @pl.when(core == 1)
    def _():
        for n, s in enumerate(far_steps):
            wo2_copy(n, z_dev(s[0]), my_quarter).start()

    def make_kv(b, carry):
        raw_kv[b] = jnp.dot(ut[256:384, :], hot[b], preferred_element_type=F32)
        return carry

    def make_q(zb, carry):
        raw_q[zb] = jnp.dot(ut[:256, :], hot[zb * 4 + x], preferred_element_type=F32)
        return carry

    lax.fori_loop(0, NCTX, make_kv, 0)
    lax.fori_loop(0, 4, make_q, 0)

    loop(1, 16, lambda i: sc_copy(i, (c - i + NCTX) % NCTX).wait_recv())

    def turn(v, b, scale_row):
        cols = pl.ds(pl.multiple_of(b * BLK, BLK), BLK)
        cos, sin = cos_ref[:, cols] * scale_row, sin_ref[:, cols] * scale_row
        lo, hi = v[:32], v[32:]
        return jnp.concatenate([lo * cos - hi * sin, hi * cos + lo * sin], axis=0)

    def turn_kv(b, carry):
        cols = pl.ds(pl.multiple_of(b * BLK, BLK), BLK)
        k_scr[pl.ds(pl.multiple_of(b * BLK, BLK), BLK), :] = (
            turn(raw_kv[b, :64], b, scale_all[b]).astype(BF16).T
        )
        vt_scr[:64, cols] = (raw_kv[b, 64:] * scale_all[b]).astype(BF16)
        return carry

    def turn_q(zb, carry):
        b = zb * 4 + x
        row = scale_all[b] * (math.log2(math.e) / math.sqrt(HD))
        for h in range(4):
            qt_scr[zb, :, h * BLK : (h + 1) * BLK] = turn(raw_q[zb, h * HD : (h + 1) * HD], b, row).astype(BF16)
        return carry

    vt_scr[64:, :] = jnp.ones_like(vt_scr[64:, :])
    for copy in late:
        copy.wait()
    lax.fori_loop(0, NCTX, turn_kv, 0)
    lax.fori_loop(0, 4, turn_q, 0)

    def scores(zb, i, h):
        keys = k_scr[pl.ds(pl.multiple_of(i * BLK, BLK), BLK), :]
        return jnp.dot(keys, qt_scr[zb, :, h * BLK : (h + 1) * BLK], preferred_element_type=F32)

    def soft(i, s, state):
        top, acc = state
        new_top = jnp.maximum(top, jnp.max(s, axis=0, keepdims=True))
        probs = jnp.exp2(s - new_top).astype(BF16)
        values = vt_scr[:, pl.ds(pl.multiple_of(i * BLK, BLK), BLK)]
        acc = acc * jnp.exp2(top - new_top) + jnp.dot(values, probs, preferred_element_type=F32)
        return new_top, acc

    key_row = lax.broadcasted_iota(jnp.int32, (BLK, BLK), 0)
    query_row = lax.broadcasted_iota(jnp.int32, (BLK, BLK), 1) + x * BLK

    def attend(zb):
        def one(i, carry, masked_block):
            states, now = carry
            later, new_states = [], []
            for h in range(4):
                if masked_block != 3:
                    later.append(scores(zb, i + 1, h))
                s = now[h]
                if masked_block is not None:
                    s = jnp.where(key_row + masked_block * BLK <= query_row, s, masked_score)
                new_states.append(soft(i, s, states[h]))
            return new_states, later

        def four(j, carry):
            for k in range(4):
                carry = one(j * 4 + k, carry, None)
            return carry

        carry = (
            [(jnp.full((1, BLK), masked_score, F32), jnp.zeros((80, BLK), F32)) for _ in range(4)],
            [scores(zb, 0, h) for h in range(4)],
        )
        for j in range(zb):
            carry = four(j, carry)
        for k in range(4):
            carry = one(4 * zb + k, carry, k)
        for h in range(4):
            _, acc = carry[0][h]
            att_out[zb, h * HD : (h + 1) * HD] = (acc[:HD] / acc[HD : HD + 1]).astype(BF16)

    def att_copy(zb, slot):
        return rc(att_out.at[zb], att_in.at[slot], at_s.at[zb], at_r.at[slot], (f, zb * 4 + x))

    def block_step(i, carry):
        zb = (zl + i) % 4

        @pl.when(i == 3)
        def _():
            for n, s in enumerate(far_steps):
                wo2_copy(n, x_dev(s[0]), (my_quarter - s[0] + 4) % 4).wait_recv()
            rc(wo.at[:, :, core], wo.at[:, :, core], wo3_s.at[0], wo3_r.at[0], (sib, c)).start()

        for k in range(4):

            @pl.when(zb == k)
            def _():
                attend(k)

        @pl.when(i < 4)
        def _():
            att_copy(zb, zl).start()

        return carry

    lax.fori_loop(1, 5, block_step, 0)
    att_in[zl] = att_out[zl]

    @pl.when(at_edge)
    def _():
        for t in (1, 2):
            wq_near(t, y * 2 + zh).wait_send()
            wo_near(t, y * 2 + zh).wait_send()

    loop(1, 16, lambda i: sc_copy(i, c).wait_send())
    for half_z in (0, 1):
        loop(1, 8, lambda i: wg_copy(i, y, half_z).wait_send())
        loop(1, 8, lambda i: wo_copy(i, y, half_z).wait_send())

    for n, s in enumerate(far_steps):
        wo2_copy(n, x_dev(s[0]), my_quarter).wait_send()
    for n in range(6):
        along_x(n, 0).wait_send()
    for n in range(4):
        over(n, slice_x(0, core)).wait_send()
    rc(wg.at[:, core], wg.at[:, core], wgx_s.at[0], wgx_r.at[0], (sib, c)).wait_send()

    ref = wo.at[:, :, 1 - core]
    rc(ref, ref, wo3_s.at[0], wo3_r.at[0], (sib, c)).wait_recv()
    for i in (1, 2, 3):
        slot = (zl - i + 4) % 4
        att_copy(slot, slot).wait_recv()

    attended = att_in[...].reshape(D, BLK).T
    pick = (align_ref[...] - c * BLK == lax.broadcasted_iota(jnp.int32, (BLK, BLK), 0)).astype(BF16)
    total = jnp.zeros((BLK, 1), F32)
    for j in range(4):
        cols = pl.ds(j * 256, 256)
        branch = jnp.dot(attended, wo[j].reshape(D, 256), preferred_element_type=F32)
        hidden = (lat_scr[:, cols].astype(F32) + branch).astype(BF16)
        hid_ref[:, cols] = hidden
        diff = tn(pick, hidden) - teach_ref[:, cols].astype(F32)
        total = total + jnp.sum(diff * diff, axis=1, keepdims=True)
    loss_ref[...] = jnp.broadcast_to(total * (1.0 / D), (BLK, 128)).T[0:1, :]

    rc(wo.at[:, :, core], wo.at[:, :, core], wo3_s.at[0], wo3_r.at[0], (sib, c)).wait_send()
    for i in (1, 2, 3):
        att_copy((zl + i) % 4, zl).wait_send()


def body(byte_ids, byte_table, w_conv, w_qkv, w_out, norm_gain, teacher, align):
    cos, sin = rope_tables(NCTX * BLK)
    vm = pl.BlockSpec(memory_space=pltpu.VMEM)
    dma = pltpu.SemaphoreType.DMA
    hidden, loss = pl.pallas_call(
        kernel,
        out_shape=(
            jax.ShapeDtypeStruct((BLK, D), BF16),
            jax.ShapeDtypeStruct((1, BLK), F32),
        ),
        in_specs=[vm] * 6 + [pl.BlockSpec(memory_space=pl.ANY)] * 3 + [vm],
        out_specs=(vm, vm),
        scratch_shapes=[
            pltpu.VMEM((3, 48, 128), BF16),
            pltpu.VMEM((3, 32, 384), BF16),
            pltpu.VMEM((NCTX, KW, BLK), jnp.int32),
            pltpu.VMEM((NCTX, 1, BLK), F32),
            pltpu.VMEM((8, 48, 128), BF16),
            pltpu.VMEM((2, 4, 4, 64, 512), BF16),
            pltpu.VMEM((16, 2, 32, 384), BF16),
            pltpu.VMEM((4, 16, 2, 32, 256), BF16),
            pltpu.VMEM((384, 1024), BF16),
            pltpu.VMEM((NCTX * BLK, HD), BF16),
            pltpu.VMEM((80, NCTX * BLK), BF16),
            pltpu.VMEM((4, HD, 4 * BLK), BF16),
            pltpu.VMEM((BLK, D), BF16),
            pltpu.VMEM((4, BLK, BLK), BF16),
            pltpu.VMEM((4, BLK, BLK), BF16),
            pltpu.VMEM((128, 128), F32),
            pltpu.VMEM((NCTX, D, BLK), BF16),
            pltpu.VMEM((NCTX, 128, BLK), F32),
            pltpu.VMEM((4, BLK, BLK), F32),
            pltpu.VMEM((D, BLK), F32),
            pltpu.VMEM((HD // 2, NCTX * BLK), F32),
            pltpu.VMEM((HD // 2, NCTX * BLK), F32),
            pltpu.VMEM((BLK, D), BF16),
            pltpu.SemaphoreType.DMA((3,)),
        ]
        + [
            dma((n,))
            for n in (16, 16, 16, 16, 12, 8, 4, 4, 3, 3, 6, 6, 4, 4, 18, 17, 1, 1, 18, 17, 4, 4, 1, 1, 4, 4)
        ],
        compiler_params=pltpu.CompilerParams(
            collective_id=0, has_side_effects=True, vmem_limit_bytes=56 * 2**20
        ),
    )(byte_ids, byte_table, w_conv, w_qkv, w_out, norm_gain.reshape(8, 128), jnp.asarray(cos), jnp.asarray(sin), teacher[0], align)
    return hidden[None], loss


def solution(mesh):
    in_specs = (
        P("fsdp", "ctx"),
        P(),
        P("fsdp", None),
        P("fsdp", None),
        P("fsdp", None),
        P(),
        P("fsdp", "ctx", None),
        P("fsdp", "ctx"),
    )
    out_specs = (P("fsdp", "ctx", None), P("fsdp", "ctx"))
    return jax.shard_map(body, mesh=mesh, in_specs=in_specs, out_specs=out_specs, check_vma=False)
```

```python
import math

import jax
import jax.numpy as jnp
import numpy as np
from jax import lax
from jax.experimental import pallas as pl
from jax.experimental.pallas import tpu as pltpu
from jax.sharding import PartitionSpec as P

KW = 4
HQ = 16
HK = 4
HD = 64
D = 1024
BLK = 256
NCTX = 16
theta_base = 500000.0
norm_eps = 1e-05
masked_score = -1e30
MESH = pl.DeviceIdType.MESH
F32 = jnp.float32
BF16 = jnp.bfloat16


def rope_tables(length):
    half = HD // 2
    frequency = theta_base ** (-np.arange(half, dtype=np.float64) * 2.0 / HD)
    angles = frequency[:, None] * np.arange(length, dtype=np.float64)[None, :]
    return np.cos(angles).astype(np.float32), np.sin(angles).astype(np.float32)


def rc(src, dst, send, recv, dev):
    return pltpu.make_async_remote_copy(
        src_ref=src, dst_ref=dst, send_sem=send, recv_sem=recv, device_id=dev, device_id_type=MESH
    )


def tn(a, b):
    return lax.dot_general(a, b, (((0,), (0,)), ((), ())), preferred_element_type=F32)


def kernel(
    ids_ref, bt_ref, wconv_ref, wqkv_ref, wo_ref, gain_ref, cos_hbm, sin_hbm, teach_hbm, align_ref,
    hid_ref, loss_ref,
    wc_src, wq_src, ids_all, scale_all, wc_all, tt, wg, wo, ut, k_scr, vt_scr, qt_scr, lat_scr, att_out, att_in,
    gain_scr, hot, raw_kv, raw_q, lat_acc, cos_ref, sin_ref, teach_ref, in_s,
    ids_s, ids_r, sc_s, sc_r, wc_s, wc_r, ty_s, ty_r, t3_s, t3_r, t4_s, t4_r, t5_s, t5_r,
    wg_s, wg_r, wgx_s, wgx_r, wo_s, wo_r, wo2_s, wo2_r, wo3_s, wo3_r, at_s, at_r,
):
    f = lax.axis_index("fsdp")
    c = lax.axis_index("ctx")
    core = f % 2
    y, zh = f // 4, (f // 2) % 2
    zl, x = c // 4, c % 4
    tap = f // 8
    sib = (f // 2) * 2 + 1 - core
    zfull = zh * 4 + zl
    steps = (1, -1, 2)

    def loop(lo, hi, fn):
        def step(i, carry):
            fn(i)
            return carry

        lax.fori_loop(lo, hi, step, 0)

    def ctx_peer(i):
        return (f, (c + i) % NCTX)

    def y_peer(i):
        return (((y + i) % 8) * 4 + zh * 2 + core, c)

    def mate_row(d):
        return y - y % 2 + (y + d // 2) % 2

    def block_dev(step, d):
        z2 = (zfull + step + 8) % 8
        return (mate_row(d) * 4 + (z2 // 4) * 2 + (core + d) % 2, (z2 % 4) * 4 + x)

    def z_dev(step):
        return block_dev(step, 0)

    def x_dev(step):
        return (f, zl * 4 + (x + step + 4) % 4)

    barrier = pltpu.get_barrier_semaphore()

    def sig(dev):
        pl.semaphore_signal(barrier, inc=1, device_id=dev, device_id_type=MESH)

    for d in range(4):
        for step in (1, -1, 2, -2):
            sig(block_dev(step, d))
    for d in range(1, 4):
        sig(block_dev(0, d))
    loop(1, 8, lambda i: sig(y_peer(i)))
    loop(1, 16, lambda i: sig(ctx_peer(i)))

    reach = jnp.where(zl == 3, 1, -1)
    at_edge = (zl == 3) | (zl == 0)

    def pack_conv(slot, z):
        col = z * 4 + x
        both = wconv_ref[:, pl.ds(pl.multiple_of(col // 2 * 128, 128), 128)]
        mine = jnp.where(col % 2 == 0, both[:, :64], both[:, 64:])
        wc_src[slot] = jnp.concatenate([mine[:48], mine[48:]], axis=1)

    def mate_slot(d, half_z):
        return (y + d // 2) % 2 * 4 + half_z * 2 + (core + d) % 2

    my_slot = mate_slot(0, zh)
    pack_conv(0, zl)
    for t in (1, 2):
        pack_conv(t, (zl + reach * t + 4) % 4)
    wc_all[my_slot] = wc_src[0]
    pl.semaphore_wait(barrier, 16 + 3 + 7 + 15)

    def wc_copy(d, slot):
        return rc(wc_src.at[0], wc_all.at[slot], wc_s.at[d], wc_r.at[d], block_dev(0, d))

    def wc_near(t, d, slot):
        return rc(
            wc_src.at[t], wc_all.at[slot], wc_s.at[4 * t + d], wc_r.at[4 + d], block_dev(reach * t, d)
        )

    @pl.when(at_edge)
    def _():
        for t in (1, 2):
            for d in range(4):
                wc_near(t, d, my_slot).start()

    for d in range(1, 4):
        wc_copy(d, my_slot).start()

    late = [
        pltpu.make_async_copy(src, dst, in_s.at[n])
        for n, (src, dst) in enumerate(((cos_hbm, cos_ref), (sin_hbm, sin_ref), (teach_hbm, teach_ref)))
    ]
    for copy in late:
        copy.start()

    taps = lax.broadcasted_iota(jnp.int32, (8, 4 * BLK), 0)
    at = lax.broadcasted_iota(jnp.int32, (8, 4 * BLK), 1)
    spread = jnp.where(at % KW == taps, jnp.broadcast_to(ids_ref[...], (8, 4 * BLK)).astype(F32), 0.0)
    to_row = lax.broadcasted_iota(jnp.int32, (4 * BLK, BLK), 0) // KW
    to_row = (to_row == lax.broadcasted_iota(jnp.int32, (4 * BLK, BLK), 1)).astype(BF16)
    rows_of = jnp.dot(spread.astype(BF16), to_row, preferred_element_type=F32)
    ids_all[c] = rows_of[:KW].astype(jnp.int32)

    def ids_copy(i, slot):
        ref = ids_all.at[slot]
        return rc(ref, ref, ids_s.at[i], ids_r.at[i], ctx_peer(i))

    gains = gain_ref[...].astype(F32)
    here = lax.broadcasted_iota(jnp.int32, (8, 128), 0) == f // 4
    gains = jnp.sum(jnp.where(here, gains, 0.0), axis=0, keepdims=True)
    gain_scr[...] = jnp.broadcast_to(gains, (128, 128)).T
    my_gain = gain_scr[pl.ds(pl.multiple_of(f % 4 * 32, 32), 32), 0:1]

    def pack_heads(slot, z):
        def heads_of(start):
            two = wqkv_ref[:, pl.ds(pl.multiple_of(start + z // 2 * 128, 128), 128)]
            return jnp.where(z % 2 == 0, two[:, :64], two[:, 64:])

        mine = jnp.concatenate(
            [wqkv_ref[:, pl.ds(pl.multiple_of(z * 256, 256), 256)], heads_of(HQ * HD), heads_of((HQ + HK) * HD)],
            axis=1,
        )
        wq_src[slot] = (mine.astype(F32) * my_gain).astype(BF16)

    pack_heads(0, zl)
    for t in (1, 2):
        pack_heads(t, (zl + reach * t + 4) % 4)
    wg[y * 2 + zh, core] = wq_src[0]

    def quarter(z):
        return jnp.where(core == 0, x, z)

    def wo_cols(z):
        return wo_ref.at[:, pl.ds(pl.multiple_of(quarter(z) * 256, 256), 256)]

    my_quarter = quarter(zl)
    wo[my_quarter, y * 2 + zh, core] = wo_ref[:, pl.ds(pl.multiple_of(my_quarter * 256, 256), 256)]

    def wq_near(t, slot):
        return rc(wq_src.at[t], wg.at[slot, core], wg_s.at[15 + t], wg_r.at[16], z_dev(reach * t))

    def wo_near(t, slot):
        z = (zl + reach * t + 4) % 4
        return rc(wo_cols(z), wo.at[quarter(z), slot, core], wo_s.at[15 + t], wo_r.at[16], z_dev(reach * t))

    @pl.when(at_edge)
    def _():
        for t in (1, 2):
            wq_near(t, y * 2 + zh).start()
            wo_near(t, y * 2 + zh).start()

    loop(1, 16, lambda i: ids_copy(i, c).start())

    def wg_copy(i, row, half_z):
        ref = wg.at[row * 2 + half_z, core]
        n = i + 8 * jnp.where(half_z == zh, 0, 1)
        return rc(ref, ref, wg_s.at[n], wg_r.at[n], y_peer(i))

    def wo_copy(i, row, half_z):
        ref = wo.at[my_quarter, row * 2 + half_z, core]
        n = i + 8 * jnp.where(half_z == zh, 0, 1)
        return rc(ref, ref, wo_s.at[n], wo_r.at[n], y_peer(i))

    loop(1, 8, lambda i: wg_copy(i, y, zh).start())

    btt = bt_ref[...].T
    bta = jnp.concatenate([btt[m * 96 : m * 96 + 48] for m in range(8)], axis=0)
    btb = jnp.concatenate([btt[m * 96 + 48 : m * 96 + 96] for m in range(8)], axis=0)

    for d in range(1, 4):
        wc_copy(d, mate_slot(d, zh)).wait_recv()
    for d in range(4):
        wc_near(1, d, mate_slot(d, 1 - zh)).wait_recv()
    wc_val = wc_all[...].reshape(384, 128)
    piece = tn(wc_val, bta)[:64] + tn(wc_val, btb)[64:]

    away = jnp.where(y % 2 == 0, -1, 1)

    def y_copy(step, from_tap):
        ref = tt.at[core, zl, x, :, pl.ds(pl.multiple_of(from_tap % 2 * 256, 256), 256)]
        return rc(ref, ref, ty_s.at[step], ty_r.at[step], y_peer(8 + away * step))

    @pl.when(tap // 2 == core)
    def _():
        tt[core, zl, x, :, pl.ds(pl.multiple_of(tap % 2 * 256, 256), 256)] = piece.astype(BF16)
        for step in (1, 2, 3):
            y_copy(step, tap).start()

    wq_near(1, y * 2 + 1 - zh).wait_recv()
    loop(1, 8, lambda i: wg_copy(i, y, 1 - zh).start())

    for step in (1, 2, 3):
        src_tap = (tap + (away, -away, 2)[step - 1] + 4) % 4

        @pl.when(src_tap // 2 == core)
        def _():
            y_copy(step, src_tap).wait_recv()

    own = tt.at[core, zl, x]

    def first_copy(n, dev, ref):
        return rc(ref, ref, t3_s.at[n], t3_r.at[n], dev)

    ways = (1, -1, 1, -1, 1, -1)
    parts = (0, 2, 2, 0, 0, 2)

    def along_x(n, shift):
        ref = tt.at[core, pl.ds(parts[n], 2), (x + shift + 4) % 4]
        return rc(ref, ref, t4_s.at[n], t4_r.at[n], x_dev(ways[n]))

    def along_z(n, shift):
        ref = tt.at[core, (zl + shift + 4) % 4, pl.ds(parts[n], 2)]
        return rc(ref, ref, t4_s.at[n], t4_r.at[n], z_dev(ways[n]))

    def make_hot(b, carry):
        rows = lax.broadcasted_iota(jnp.int32, (256, BLK), 0)
        block = ids_all[b]
        for k in range(KW):
            hot[b, k * 256 : (k + 1) * 256] = (block[k : k + 1, :] == rows).astype(BF16)
        return carry

    def meanwhile():
        rc(
            wo_cols(zl), wo.at[my_quarter, y * 2 + 1 - zh, core], wo_s.at[16], wo_r.at[16], z_dev(1)
        ).wait_recv()
        loop(1, 8, lambda i: wo_copy(i, y, 1 - zh).start())

        loop(1, 16, lambda i: ids_copy(i, (c - i + NCTX) % NCTX).wait_recv())
        lax.fori_loop(0, NCTX, make_hot, 0)
        for d in range(1, 4):
            wc_copy(d, my_slot).wait_send()

        @pl.when(at_edge)
        def _():
            for t in (1, 2):
                for d in range(4):
                    wc_near(t, d, my_slot).wait_send()

        loop(1, 16, lambda i: ids_copy(i, c).wait_send())

        @pl.when(tap // 2 == core)
        def _():
            for step in (1, 2, 3):
                y_copy(step, tap).wait_send()

        for n, s in enumerate(steps):
            first_copy(n, z_dev(s), own).wait_send()

    def over(n, ref):
        return rc(ref, ref, t5_s.at[n], t5_r.at[n], (sib, c))

    def second_axis(along, slice_of):
        over(0, slice_of(0, core)).start()
        along(0, -1).wait_recv()
        along(4, -1).start()
        along(1, 1).wait_recv()
        along(5, 1).start()
        meanwhile()
        along(2, -1).wait_recv()
        over(1, slice_of(-1, core)).start()
        along(3, 1).wait_recv()
        over(2, slice_of(1, core)).start()
        along(4, -2).wait_recv()
        along(5, 2).wait_recv()
        over(3, slice_of(2, core)).start()

    def slice_x(shift, part):
        return tt.at[part, :, (x + shift + 4) % 4]

    def slice_z(shift, part):
        return tt.at[part, (zl + shift + 4) % 4]

    @pl.when(core == 0)
    def _():
        for n, s in enumerate(steps):
            first_copy(n, z_dev(s), own).start()
        loop(1, 8, lambda i: wo_copy(i, y, zh).start())
        for n, s in enumerate(steps):
            first_copy(n, z_dev(s), tt.at[core, (zl - s + 4) % 4, x]).wait_recv()
        for n in (0, 1, 2, 3):
            along_x(n, 0).start()

    @pl.when(core == 1)
    def _():
        for n, s in enumerate(steps):
            first_copy(n, x_dev(s), own).start()
        loop(1, 8, lambda i: wo_copy(i, y, zh).start())
        for n, s in enumerate(steps):
            first_copy(n, x_dev(s), tt.at[core, zl, (x - s + 4) % 4]).wait_recv()
        for n in (0, 1, 2, 3):
            along_z(n, 0).start()

    @pl.when(core == 0)
    def _():
        second_axis(along_x, slice_x)

    @pl.when(core == 1)
    def _():
        second_axis(along_z, slice_z)

    for half_z in (0, 1):
        loop(1, 8, lambda i: wg_copy(i, (y - i + 8) % 8, half_z).wait_recv())
    rc(wg.at[:, core], wg.at[:, core], wgx_s.at[0], wgx_r.at[0], (sib, c)).start()

    def table(part):
        return tt[part].reshape(D, 512)

    def hot_rows(b, part):
        return hot[b, pl.ds(pl.multiple_of(part * 512, 512), 512)]

    lat_acc[...] = jnp.dot(table(core), hot_rows(c, core), preferred_element_type=F32)

    @pl.when(core == 0)
    def _():
        for n, shift in enumerate((0, -1, 1, 2)):
            over(n, slice_z(shift, 1 - core)).wait_recv()

    @pl.when(core == 1)
    def _():
        for n, shift in enumerate((0, -1, 1, 2)):
            over(n, slice_x(shift, 1 - core)).wait_recv()

    latent = lat_acc[...] + jnp.dot(table(1 - core), hot_rows(c, 1 - core), preferred_element_type=F32)
    latent = latent.astype(BF16)
    wide = latent.astype(F32)
    scale = lax.rsqrt(jnp.sum(wide * wide, axis=0, keepdims=True) * (1.0 / D) + norm_eps)
    scale_all[c] = scale

    def sc_copy(i, slot):
        ref = scale_all.at[slot]
        return rc(ref, ref, sc_s.at[i], sc_r.at[i], ctx_peer(i))

    loop(1, 16, lambda i: sc_copy(i, c).start())
    lat_scr[...] = latent.T

    ref = wg.at[:, 1 - core]
    rc(ref, ref, wgx_s.at[0], wgx_r.at[0], (sib, c)).wait_recv()
    wgt = wg[...].reshape(D, 384)
    for part in (0, 1):
        ut[:, part * 512 : (part + 1) * 512] = tn(wgt, table(part)).astype(BF16)

    for half_z in (0, 1):
        loop(1, 8, lambda i: wo_copy(i, (y - i + 8) % 8, half_z).wait_recv())
    far_steps = ((1, 0, 16), (-1, 0, 16), (2, 0, 8), (-2, 8, 8))

    def wo2_copy(n, dev, slot):
        ref = wo.at[slot, pl.ds(far_steps[n][1], far_steps[n][2]), core]
        return rc(ref, ref, wo2_s.at[n], wo2_r.at[n], dev)

    @pl.when(core == 0)
    def _():
        for n, s in enumerate(far_steps):
            wo2_copy(n, x_dev(s[0]), my_quarter).start()

    @pl.when(core == 1)
    def _():
        for n, s in enumerate(far_steps):
            wo2_copy(n, z_dev(s[0]), my_quarter).start()

    def make_kv(b, carry):
        raw_kv[b] = jnp.dot(ut[256:384, :], hot[b], preferred_element_type=F32)
        return carry

    def make_q(zb, carry):
        raw_q[zb] = jnp.dot(ut[:256, :], hot[zb * 4 + x], preferred_element_type=F32)
        return carry

    lax.fori_loop(0, NCTX, make_kv, 0)
    lax.fori_loop(0, 4, make_q, 0)

    loop(1, 16, lambda i: sc_copy(i, (c - i + NCTX) % NCTX).wait_recv())

    def turn(v, b, scale_row):
        cols = pl.ds(pl.multiple_of(b * BLK, BLK), BLK)
        cos, sin = cos_ref[:, cols] * scale_row, sin_ref[:, cols] * scale_row
        lo, hi = v[:32], v[32:]
        return jnp.concatenate([lo * cos - hi * sin, hi * cos + lo * sin], axis=0)

    def turn_kv(b, carry):
        cols = pl.ds(pl.multiple_of(b * BLK, BLK), BLK)
        k_scr[pl.ds(pl.multiple_of(b * BLK, BLK), BLK), :] = (
            turn(raw_kv[b, :64], b, scale_all[b]).astype(BF16).T
        )
        vt_scr[:64, cols] = (raw_kv[b, 64:] * scale_all[b]).astype(BF16)
        return carry

    def turn_q(zb, carry):
        b = zb * 4 + x
        row = scale_all[b] * (math.log2(math.e) / math.sqrt(HD))
        for h in range(4):
            qt_scr[zb, :, h * BLK : (h + 1) * BLK] = turn(raw_q[zb, h * HD : (h + 1) * HD], b, row).astype(BF16)
        return carry

    vt_scr[64:, :] = jnp.ones_like(vt_scr[64:, :])
    for copy in late:
        copy.wait()
    lax.fori_loop(0, NCTX, turn_kv, 0)
    lax.fori_loop(0, 4, turn_q, 0)

    def scores(zb, i, h):
        keys = k_scr[pl.ds(pl.multiple_of(i * BLK, BLK), BLK), :]
        return jnp.dot(keys, qt_scr[zb, :, h * BLK : (h + 1) * BLK], preferred_element_type=F32)

    def soft(i, s, state):
        top, acc = state
        new_top = jnp.maximum(top, jnp.max(s, axis=0, keepdims=True))
        probs = jnp.exp2(s - new_top).astype(BF16)
        values = vt_scr[:, pl.ds(pl.multiple_of(i * BLK, BLK), BLK)]
        acc = acc * jnp.exp2(top - new_top) + jnp.dot(values, probs, preferred_element_type=F32)
        return new_top, acc

    key_row = lax.broadcasted_iota(jnp.int32, (BLK, BLK), 0)
    query_row = lax.broadcasted_iota(jnp.int32, (BLK, BLK), 1) + x * BLK

    def attend(zb):
        def one(i, carry, masked_block):
            states, now = carry
            later, new_states = [], []
            for h in range(4):
                if masked_block != 3:
                    later.append(scores(zb, i + 1, h))
                s = now[h]
                if masked_block is not None:
                    s = jnp.where(key_row + masked_block * BLK <= query_row, s, masked_score)
                new_states.append(soft(i, s, states[h]))
            return new_states, later

        def four(j, carry):
            for k in range(4):
                carry = one(j * 4 + k, carry, None)
            return carry

        carry = (
            [(jnp.full((1, BLK), masked_score, F32), jnp.zeros((80, BLK), F32)) for _ in range(4)],
            [scores(zb, 0, h) for h in range(4)],
        )
        for j in range(zb):
            carry = four(j, carry)
        for k in range(4):
            carry = one(4 * zb + k, carry, k)
        for h in range(4):
            _, acc = carry[0][h]
            att_out[zb, h * HD : (h + 1) * HD] = (acc[:HD] / acc[HD : HD + 1]).astype(BF16)

    def att_copy(zb, slot):
        return rc(att_out.at[zb], att_in.at[slot], at_s.at[zb], at_r.at[slot], (f, zb * 4 + x))

    def block_step(i, carry):
        zb = (zl - i + 8) % 4

        @pl.when(i == 3)
        def _():
            for n, s in enumerate(far_steps):
                wo2_copy(n, x_dev(s[0]), (my_quarter - s[0] + 4) % 4).wait_recv()
            rc(wo.at[:, :, core], wo.at[:, :, core], wo3_s.at[0], wo3_r.at[0], (sib, c)).start()

        for k in range(4):

            @pl.when(zb == k)
            def _():
                attend(k)

        @pl.when(i < 4)
        def _():
            att_copy(zb, zl).start()

        return carry

    lax.fori_loop(1, 5, block_step, 0)
    att_in[zl] = att_out[zl]

    @pl.when(at_edge)
    def _():
        for t in (1, 2):
            wq_near(t, y * 2 + zh).wait_send()
            wo_near(t, y * 2 + zh).wait_send()

    loop(1, 16, lambda i: sc_copy(i, c).wait_send())
    for half_z in (0, 1):
        loop(1, 8, lambda i: wg_copy(i, y, half_z).wait_send())
        loop(1, 8, lambda i: wo_copy(i, y, half_z).wait_send())

    for n, s in enumerate(far_steps):
        wo2_copy(n, x_dev(s[0]), my_quarter).wait_send()
    for n in range(6):
        along_x(n, 0).wait_send()
    for n in range(4):
        over(n, slice_x(0, core)).wait_send()
    rc(wg.at[:, core], wg.at[:, core], wgx_s.at[0], wgx_r.at[0], (sib, c)).wait_send()

    ref = wo.at[:, :, 1 - core]
    rc(ref, ref, wo3_s.at[0], wo3_r.at[0], (sib, c)).wait_recv()
    for i in (1, 2, 3):
        slot = (zl - i + 4) % 4
        att_copy(slot, slot).wait_recv()

    attended = att_in[...].reshape(D, BLK).T
    pick = (align_ref[...] - c * BLK == lax.broadcasted_iota(jnp.int32, (BLK, BLK), 0)).astype(BF16)
    total = jnp.zeros((BLK, 1), F32)
    for j in range(4):
        cols = pl.ds(j * 256, 256)
        branch = jnp.dot(attended, wo[j].reshape(D, 256), preferred_element_type=F32)
        hidden = (lat_scr[:, cols].astype(F32) + branch).astype(BF16)
        hid_ref[:, cols] = hidden
        diff = tn(pick, hidden) - teach_ref[:, cols].astype(F32)
        total = total + jnp.sum(diff * diff, axis=1, keepdims=True)
    loss_ref[...] = jnp.broadcast_to(total * (1.0 / D), (BLK, 128)).T[0:1, :]

    rc(wo.at[:, :, core], wo.at[:, :, core], wo3_s.at[0], wo3_r.at[0], (sib, c)).wait_send()
    for i in (1, 2, 3):
        att_copy((zl + i) % 4, zl).wait_send()


def body(byte_ids, byte_table, w_conv, w_qkv, w_out, norm_gain, teacher, align):
    cos, sin = rope_tables(NCTX * BLK)
    vm = pl.BlockSpec(memory_space=pltpu.VMEM)
    dma = pltpu.SemaphoreType.DMA
    hidden, loss = pl.pallas_call(
        kernel,
        out_shape=(
            jax.ShapeDtypeStruct((BLK, D), BF16),
            jax.ShapeDtypeStruct((1, BLK), F32),
        ),
        in_specs=[vm] * 6 + [pl.BlockSpec(memory_space=pl.ANY)] * 3 + [vm],
        out_specs=(vm, vm),
        scratch_shapes=[
            pltpu.VMEM((3, 48, 128), BF16),
            pltpu.VMEM((3, 32, 384), BF16),
            pltpu.VMEM((NCTX, KW, BLK), jnp.int32),
            pltpu.VMEM((NCTX, 1, BLK), F32),
            pltpu.VMEM((8, 48, 128), BF16),
            pltpu.VMEM((2, 4, 4, 64, 512), BF16),
            pltpu.VMEM((16, 2, 32, 384), BF16),
            pltpu.VMEM((4, 16, 2, 32, 256), BF16),
            pltpu.VMEM((384, 1024), BF16),
            pltpu.VMEM((NCTX * BLK, HD), BF16),
            pltpu.VMEM((80, NCTX * BLK), BF16),
            pltpu.VMEM((4, HD, 4 * BLK), BF16),
            pltpu.VMEM((BLK, D), BF16),
            pltpu.VMEM((4, BLK, BLK), BF16),
            pltpu.VMEM((4, BLK, BLK), BF16),
            pltpu.VMEM((128, 128), F32),
            pltpu.VMEM((NCTX, D, BLK), BF16),
            pltpu.VMEM((NCTX, 128, BLK), F32),
            pltpu.VMEM((4, BLK, BLK), F32),
            pltpu.VMEM((D, BLK), F32),
            pltpu.VMEM((HD // 2, NCTX * BLK), F32),
            pltpu.VMEM((HD // 2, NCTX * BLK), F32),
            pltpu.VMEM((BLK, D), BF16),
            pltpu.SemaphoreType.DMA((3,)),
        ]
        + [
            dma((n,))
            for n in (16, 16, 16, 16, 12, 8, 4, 4, 3, 3, 6, 6, 4, 4, 18, 17, 1, 1, 18, 17, 4, 4, 1, 1, 4, 4)
        ],
        compiler_params=pltpu.CompilerParams(
            collective_id=0, has_side_effects=True, vmem_limit_bytes=56 * 2**20
        ),
    )(byte_ids, byte_table, w_conv, w_qkv, w_out, norm_gain.reshape(8, 128), jnp.asarray(cos), jnp.asarray(sin), teacher[0], align)
    return hidden[None], loss


def solution(mesh):
    in_specs = (
        P("fsdp", "ctx"),
        P(),
        P("fsdp", None),
        P("fsdp", None),
        P("fsdp", None),
        P(),
        P("fsdp", "ctx", None),
        P("fsdp", "ctx"),
    )
    out_specs = (P("fsdp", "ctx", None), P("fsdp", "ctx"))
    return jax.shard_map(body, mesh=mesh, in_specs=in_specs, out_specs=out_specs, check_vma=False)
```

```python
import math

import jax
import jax.numpy as jnp
import numpy as np
from jax import lax
from jax.experimental import pallas as pl
from jax.experimental.pallas import tpu as pltpu
from jax.sharding import PartitionSpec as P

KW = 4
HQ = 16
HK = 4
HD = 64
D = 1024
BLK = 256
NCTX = 16
theta_base = 500000.0
norm_eps = 1e-05
masked_score = -1e30
MESH = pl.DeviceIdType.MESH
F32 = jnp.float32
BF16 = jnp.bfloat16


def rope_tables(length):
    half = HD // 2
    frequency = theta_base ** (-np.arange(half, dtype=np.float64) * 2.0 / HD)
    angles = frequency[:, None] * np.arange(length, dtype=np.float64)[None, :]
    return np.cos(angles).astype(np.float32), np.sin(angles).astype(np.float32)


def rc(src, dst, send, recv, dev):
    return pltpu.make_async_remote_copy(
        src_ref=src, dst_ref=dst, send_sem=send, recv_sem=recv, device_id=dev, device_id_type=MESH
    )


def tn(a, b):
    return lax.dot_general(a, b, (((0,), (0,)), ((), ())), preferred_element_type=F32)


def kernel(
    ids_ref, bt_ref, wconv_ref, wqkv_ref, wo_ref, gain_ref, cos_hbm, sin_hbm, teach_hbm, align_ref,
    hid_ref, loss_ref,
    wc_src, wq_src, ids_all, scale_all, wc_all, tt, wg, wo, ut, k_scr, vt_scr, qt_scr, lat_scr, att_out, att_in,
    gain_scr, hot, raw_kv, raw_q, lat_acc, cos_ref, sin_ref, teach_ref, in_s,
    ids_s, ids_r, sc_s, sc_r, wc_s, wc_r, ty_s, ty_r, t3_s, t3_r, t4_s, t4_r, t5_s, t5_r,
    wg_s, wg_r, wgx_s, wgx_r, wo_s, wo_r, wo2_s, wo2_r, wo3_s, wo3_r, at_s, at_r,
):
    f = lax.axis_index("fsdp")
    c = lax.axis_index("ctx")
    core = f % 2
    y, zh = f // 4, (f // 2) % 2
    zl, x = c // 4, c % 4
    tap = f // 8
    sib = (f // 2) * 2 + 1 - core
    zfull = zh * 4 + zl
    steps = (1, -1, 2)

    def loop(lo, hi, fn):
        def step(i, carry):
            fn(i)
            return carry

        lax.fori_loop(lo, hi, step, 0)

    def ctx_peer(i):
        return (f, (c + i) % NCTX)

    def y_peer(i):
        return (((y + i) % 8) * 4 + zh * 2 + core, c)

    def mate_row(d):
        return y - y % 2 + (y + d // 2) % 2

    def block_dev(step, d):
        z2 = (zfull + step + 8) % 8
        return (mate_row(d) * 4 + (z2 // 4) * 2 + (core + d) % 2, (z2 % 4) * 4 + x)

    def z_dev(step):
        return block_dev(step, 0)

    def x_dev(step):
        return (f, zl * 4 + (x + step + 4) % 4)

    barrier = pltpu.get_barrier_semaphore()

    def sig(dev):
        pl.semaphore_signal(barrier, inc=1, device_id=dev, device_id_type=MESH)

    for d in range(4):
        for step in (1, -1, 2, -2):
            sig(block_dev(step, d))
    for d in range(1, 4):
        sig(block_dev(0, d))
    loop(1, 8, lambda i: sig(y_peer(i)))
    loop(1, 16, lambda i: sig(ctx_peer(i)))

    reach = jnp.where(zl == 3, 1, -1)
    at_edge = (zl == 3) | (zl == 0)

    def pack_conv(slot, z):
        col = z * 4 + x
        both = wconv_ref[:, pl.ds(pl.multiple_of(col // 2 * 128, 128), 128)]
        mine = jnp.where(col % 2 == 0, both[:, :64], both[:, 64:])
        wc_src[slot] = jnp.concatenate([mine[:48], mine[48:]], axis=1)

    def mate_slot(d, half_z):
        return (y + d // 2) % 2 * 4 + half_z * 2 + (core + d) % 2

    my_slot = mate_slot(0, zh)
    pack_conv(0, zl)
    for t in (1, 2):
        pack_conv(t, (zl + reach * t + 4) % 4)
    wc_all[my_slot] = wc_src[0]
    pl.semaphore_wait(barrier, 16 + 3 + 7 + 15)

    def wc_copy(d, slot):
        return rc(wc_src.at[0], wc_all.at[slot], wc_s.at[d], wc_r.at[d], block_dev(0, d))

    def wc_near(t, d, slot):
        return rc(
            wc_src.at[t], wc_all.at[slot], wc_s.at[4 * t + d], wc_r.at[4 + d], block_dev(reach * t, d)
        )

    @pl.when(at_edge)
    def _():
        for t in (1, 2):
            for d in range(4):
                wc_near(t, d, my_slot).start()

    for d in range(1, 4):
        wc_copy(d, my_slot).start()

    late = [
        pltpu.make_async_copy(src, dst, in_s.at[n])
        for n, (src, dst) in enumerate(((cos_hbm, cos_ref), (sin_hbm, sin_ref), (teach_hbm, teach_ref)))
    ]
    for copy in late:
        copy.start()

    taps = lax.broadcasted_iota(jnp.int32, (8, 4 * BLK), 0)
    at = lax.broadcasted_iota(jnp.int32, (8, 4 * BLK), 1)
    spread = jnp.where(at % KW == taps, jnp.broadcast_to(ids_ref[...], (8, 4 * BLK)).astype(F32), 0.0)
    to_row = lax.broadcasted_iota(jnp.int32, (4 * BLK, BLK), 0) // KW
    to_row = (to_row == lax.broadcasted_iota(jnp.int32, (4 * BLK, BLK), 1)).astype(BF16)
    rows_of = jnp.dot(spread.astype(BF16), to_row, preferred_element_type=F32)
    ids_all[c] = rows_of[:KW].astype(jnp.int32)

    def ids_copy(i, slot):
        ref = ids_all.at[slot]
        return rc(ref, ref, ids_s.at[i], ids_r.at[i], ctx_peer(i))

    gains = gain_ref[...].astype(F32)
    here = lax.broadcasted_iota(jnp.int32, (8, 128), 0) == f // 4
    gains = jnp.sum(jnp.where(here, gains, 0.0), axis=0, keepdims=True)
    gain_scr[...] = jnp.broadcast_to(gains, (128, 128)).T
    my_gain = gain_scr[pl.ds(pl.multiple_of(f % 4 * 32, 32), 32), 0:1]

    def pack_heads(slot, z):
        def heads_of(start):
            two = wqkv_ref[:, pl.ds(pl.multiple_of(start + z // 2 * 128, 128), 128)]
            return jnp.where(z % 2 == 0, two[:, :64], two[:, 64:])

        mine = jnp.concatenate(
            [wqkv_ref[:, pl.ds(pl.multiple_of(z * 256, 256), 256)], heads_of(HQ * HD), heads_of((HQ + HK) * HD)],
            axis=1,
        )
        wq_src[slot] = (mine.astype(F32) * my_gain).astype(BF16)

    pack_heads(0, zl)
    for t in (1, 2):
        pack_heads(t, (zl + reach * t + 4) % 4)
    wg[y * 2 + zh, core] = wq_src[0]

    def quarter(z):
        return jnp.where(core == 0, x, z)

    def wo_cols(z):
        return wo_ref.at[:, pl.ds(pl.multiple_of(quarter(z) * 256, 256), 256)]

    my_quarter = quarter(zl)
    wo[my_quarter, y * 2 + zh, core] = wo_ref[:, pl.ds(pl.multiple_of(my_quarter * 256, 256), 256)]

    def wq_near(t, slot):
        return rc(wq_src.at[t], wg.at[slot, core], wg_s.at[15 + t], wg_r.at[16], z_dev(reach * t))

    def wo_near(t, slot):
        z = (zl + reach * t + 4) % 4
        return rc(wo_cols(z), wo.at[quarter(z), slot, core], wo_s.at[15 + t], wo_r.at[16], z_dev(reach * t))

    @pl.when(at_edge)
    def _():
        for t in (1, 2):
            wq_near(t, y * 2 + zh).start()
            wo_near(t, y * 2 + zh).start()

    loop(1, 16, lambda i: ids_copy(i, c).start())

    def wg_copy(i, row, half_z):
        ref = wg.at[row * 2 + half_z, core]
        n = i + 8 * jnp.where(half_z == zh, 0, 1)
        return rc(ref, ref, wg_s.at[n], wg_r.at[n], y_peer(i))

    def wo_copy(i, row, half_z):
        ref = wo.at[my_quarter, row * 2 + half_z, core]
        n = i + 8 * jnp.where(half_z == zh, 0, 1)
        return rc(ref, ref, wo_s.at[n], wo_r.at[n], y_peer(i))

    loop(1, 8, lambda i: wg_copy(i, y, zh).start())

    btt = bt_ref[...].T
    bta = jnp.concatenate([btt[m * 96 : m * 96 + 48] for m in range(8)], axis=0)
    btb = jnp.concatenate([btt[m * 96 + 48 : m * 96 + 96] for m in range(8)], axis=0)

    for d in range(1, 4):
        wc_copy(d, mate_slot(d, zh)).wait_recv()
    for d in range(4):
        wc_near(1, d, mate_slot(d, 1 - zh)).wait_recv()
    wc_val = wc_all[...].reshape(384, 128)
    piece = tn(wc_val, bta)[:64] + tn(wc_val, btb)[64:]

    away = jnp.where(y % 2 == 0, -1, 1)

    def y_copy(step, from_tap):
        ref = tt.at[core, zl, x, :, pl.ds(pl.multiple_of(from_tap % 2 * 256, 256), 256)]
        return rc(ref, ref, ty_s.at[step], ty_r.at[step], y_peer(8 + away * step))

    @pl.when(tap // 2 == core)
    def _():
        tt[core, zl, x, :, pl.ds(pl.multiple_of(tap % 2 * 256, 256), 256)] = piece.astype(BF16)
        for step in (1, 2, 3):
            y_copy(step, tap).start()

    wq_near(1, y * 2 + 1 - zh).wait_recv()
    loop(1, 8, lambda i: wg_copy(i, y, 1 - zh).start())

    for step in (1, 2, 3):
        src_tap = (tap + (away, -away, 2)[step - 1] + 4) % 4

        @pl.when(src_tap // 2 == core)
        def _():
            y_copy(step, src_tap).wait_recv()

    own = tt.at[core, zl, x]

    def first_copy(n, dev, ref):
        return rc(ref, ref, t3_s.at[n], t3_r.at[n], dev)

    ways = (1, -1, 1, -1, 1, -1)
    parts = (0, 2, 2, 0, 0, 2)

    def along_x(n, shift):
        ref = tt.at[core, pl.ds(parts[n], 2), (x + shift + 4) % 4]
        return rc(ref, ref, t4_s.at[n], t4_r.at[n], x_dev(ways[n]))

    def along_z(n, shift):
        ref = tt.at[core, (zl + shift + 4) % 4, pl.ds(parts[n], 2)]
        return rc(ref, ref, t4_s.at[n], t4_r.at[n], z_dev(ways[n]))

    def make_hot(b, carry):
        rows = lax.broadcasted_iota(jnp.int32, (256, BLK), 0)
        block = ids_all[b]
        for k in range(KW):
            hot[b, k * 256 : (k + 1) * 256] = (block[k : k + 1, :] == rows).astype(BF16)
        return carry

    def meanwhile():
        rc(
            wo_cols(zl), wo.at[my_quarter, y * 2 + 1 - zh, core], wo_s.at[16], wo_r.at[16], z_dev(1)
        ).wait_recv()
        loop(1, 8, lambda i: wo_copy(i, y, 1 - zh).start())

        loop(1, 16, lambda i: ids_copy(i, (c - i + NCTX) % NCTX).wait_recv())
        lax.fori_loop(0, NCTX, make_hot, 0)
        for d in range(1, 4):
            wc_copy(d, my_slot).wait_send()

        @pl.when(at_edge)
        def _():
            for t in (1, 2):
                for d in range(4):
                    wc_near(t, d, my_slot).wait_send()

        loop(1, 16, lambda i: ids_copy(i, c).wait_send())

        @pl.when(tap // 2 == core)
        def _():
            for step in (1, 2, 3):
                y_copy(step, tap).wait_send()

        for n, s in enumerate(steps):
            first_copy(n, z_dev(s), own).wait_send()

    def over(n, ref):
        return rc(ref, ref, t5_s.at[n], t5_r.at[n], (sib, c))

    def second_axis(along, slice_of):
        over(0, slice_of(0, core)).start()
        along(0, -1).wait_recv()
        along(4, -1).start()
        along(1, 1).wait_recv()
        along(5, 1).start()
        meanwhile()
        along(2, -1).wait_recv()
        over(1, slice_of(-1, core)).start()
        along(3, 1).wait_recv()
        over(2, slice_of(1, core)).start()
        along(4, -2).wait_recv()
        along(5, 2).wait_recv()
        over(3, slice_of(2, core)).start()

    def slice_x(shift, part):
        return tt.at[part, :, (x + shift + 4) % 4]

    def slice_z(shift, part):
        return tt.at[part, (zl + shift + 4) % 4]

    @pl.when(core == 0)
    def _():
        for n, s in enumerate(steps):
            first_copy(n, z_dev(s), own).start()
        loop(1, 8, lambda i: wo_copy(i, y, zh).start())
        for n, s in enumerate(steps):
            first_copy(n, z_dev(s), tt.at[core, (zl - s + 4) % 4, x]).wait_recv()
        for n in (0, 1, 2, 3):
            along_x(n, 0).start()

    @pl.when(core == 1)
    def _():
        for n, s in enumerate(steps):
            first_copy(n, x_dev(s), own).start()
        loop(1, 8, lambda i: wo_copy(i, y, zh).start())
        for n, s in enumerate(steps):
            first_copy(n, x_dev(s), tt.at[core, zl, (x - s + 4) % 4]).wait_recv()
        for n in (0, 1, 2, 3):
            along_z(n, 0).start()

    @pl.when(core == 0)
    def _():
        second_axis(along_x, slice_x)

    @pl.when(core == 1)
    def _():
        second_axis(along_z, slice_z)

    for half_z in (0, 1):
        loop(1, 8, lambda i: wg_copy(i, (y - i + 8) % 8, half_z).wait_recv())
    rc(wg.at[:, core], wg.at[:, core], wgx_s.at[0], wgx_r.at[0], (sib, c)).start()

    def table(part):
        return tt[part].reshape(D, 512)

    def hot_rows(b, part):
        return hot[b, pl.ds(pl.multiple_of(part * 512, 512), 512)]

    lat_acc[...] = jnp.dot(table(core), hot_rows(c, core), preferred_element_type=F32)

    @pl.when(core == 0)
    def _():
        for n, shift in enumerate((0, -1, 1, 2)):
            over(n, slice_z(shift, 1 - core)).wait_recv()

    @pl.when(core == 1)
    def _():
        for n, shift in enumerate((0, -1, 1, 2)):
            over(n, slice_x(shift, 1 - core)).wait_recv()

    latent = lat_acc[...] + jnp.dot(table(1 - core), hot_rows(c, 1 - core), preferred_element_type=F32)
    latent = latent.astype(BF16)
    wide = latent.astype(F32)
    scale = lax.rsqrt(jnp.sum(wide * wide, axis=0, keepdims=True) * (1.0 / D) + norm_eps)
    scale_all[c] = scale

    def sc_copy(i, slot):
        ref = scale_all.at[slot]
        return rc(ref, ref, sc_s.at[i], sc_r.at[i], ctx_peer(i))

    loop(1, 16, lambda i: sc_copy(i, c).start())
    lat_scr[...] = latent.T

    ref = wg.at[:, 1 - core]
    rc(ref, ref, wgx_s.at[0], wgx_r.at[0], (sib, c)).wait_recv()
    wgt = wg[...].reshape(D, 384).T
    for part in (0, 1):
        ut[:, part * 512 : (part + 1) * 512] = jnp.dot(wgt, table(part), preferred_element_type=F32).astype(BF16)

    for half_z in (0, 1):
        loop(1, 8, lambda i: wo_copy(i, (y - i + 8) % 8, half_z).wait_recv())
    far_steps = ((1, 0, 16), (-1, 0, 16), (2, 0, 8), (-2, 8, 8))

    def wo2_copy(n, dev, slot):
        ref = wo.at[slot, pl.ds(far_steps[n][1], far_steps[n][2]), core]
        return rc(ref, ref, wo2_s.at[n], wo2_r.at[n], dev)

    @pl.when(core == 0)
    def _():
        for n, s in enumerate(far_steps):
            wo2_copy(n, x_dev(s[0]), my_quarter).start()

    @pl.when(core == 1)
    def _():
        for n, s in enumerate(far_steps):
            wo2_copy(n, z_dev(s[0]), my_quarter).start()

    def make_kv(b, carry):
        raw_kv[b] = jnp.dot(ut[256:384, :], hot[b], preferred_element_type=F32)
        return carry

    def make_q(zb, carry):
        raw_q[zb] = jnp.dot(ut[:256, :], hot[zb * 4 + x], preferred_element_type=F32)
        return carry

    lax.fori_loop(0, NCTX, make_kv, 0)
    lax.fori_loop(0, 4, make_q, 0)

    loop(1, 16, lambda i: sc_copy(i, (c - i + NCTX) % NCTX).wait_recv())

    def turn(v, b, scale_row):
        cols = pl.ds(pl.multiple_of(b * BLK, BLK), BLK)
        cos, sin = cos_ref[:, cols] * scale_row, sin_ref[:, cols] * scale_row
        lo, hi = v[:32], v[32:]
        return jnp.concatenate([lo * cos - hi * sin, hi * cos + lo * sin], axis=0)

    def turn_kv(b, carry):
        cols = pl.ds(pl.multiple_of(b * BLK, BLK), BLK)
        k_scr[pl.ds(pl.multiple_of(b * BLK, BLK), BLK), :] = (
            turn(raw_kv[b, :64], b, scale_all[b]).astype(BF16).T
        )
        vt_scr[:64, cols] = (raw_kv[b, 64:] * scale_all[b]).astype(BF16)
        return carry

    def turn_q(zb, carry):
        b = zb * 4 + x
        row = scale_all[b] * (math.log2(math.e) / math.sqrt(HD))
        for h in range(4):
            qt_scr[zb, :, h * BLK : (h + 1) * BLK] = turn(raw_q[zb, h * HD : (h + 1) * HD], b, row).astype(BF16)
        return carry

    vt_scr[64:, :] = jnp.ones_like(vt_scr[64:, :])
    for copy in late:
        copy.wait()
    lax.fori_loop(0, NCTX, turn_kv, 0)
    lax.fori_loop(0, 4, turn_q, 0)

    def scores(zb, i, h):
        keys = k_scr[pl.ds(pl.multiple_of(i * BLK, BLK), BLK), :]
        return jnp.dot(keys, qt_scr[zb, :, h * BLK : (h + 1) * BLK], preferred_element_type=F32)

    def soft(i, s, state):
        top, acc = state
        new_top = jnp.maximum(top, jnp.max(s, axis=0, keepdims=True))
        probs = jnp.exp2(s - new_top).astype(BF16)
        values = vt_scr[:, pl.ds(pl.multiple_of(i * BLK, BLK), BLK)]
        acc = acc * jnp.exp2(top - new_top) + jnp.dot(values, probs, preferred_element_type=F32)
        return new_top, acc

    key_row = lax.broadcasted_iota(jnp.int32, (BLK, BLK), 0)
    query_row = lax.broadcasted_iota(jnp.int32, (BLK, BLK), 1) + x * BLK

    def attend(zb):
        def one(i, carry, masked_block):
            states, now = carry
            later, new_states = [], []
            for h in range(4):
                if masked_block != 3:
                    later.append(scores(zb, i + 1, h))
                s = now[h]
                if masked_block is not None:
                    s = jnp.where(key_row + masked_block * BLK <= query_row, s, masked_score)
                new_states.append(soft(i, s, states[h]))
            return new_states, later

        def four(j, carry):
            for k in range(4):
                carry = one(j * 4 + k, carry, None)
            return carry

        carry = (
            [(jnp.full((1, BLK), masked_score, F32), jnp.zeros((80, BLK), F32)) for _ in range(4)],
            [scores(zb, 0, h) for h in range(4)],
        )
        for j in range(zb):
            carry = four(j, carry)
        for k in range(4):
            carry = one(4 * zb + k, carry, k)
        for h in range(4):
            _, acc = carry[0][h]
            att_out[zb, h * HD : (h + 1) * HD] = (acc[:HD] / acc[HD : HD + 1]).astype(BF16)

    def att_copy(zb, slot):
        return rc(att_out.at[zb], att_in.at[slot], at_s.at[zb], at_r.at[slot], (f, zb * 4 + x))

    def block_step(i, carry):
        zb = (zl - i + 8) % 4

        @pl.when(i == 3)
        def _():
            for n, s in enumerate(far_steps):
                wo2_copy(n, x_dev(s[0]), (my_quarter - s[0] + 4) % 4).wait_recv()
            rc(wo.at[:, :, core], wo.at[:, :, core], wo3_s.at[0], wo3_r.at[0], (sib, c)).start()

        for k in range(4):

            @pl.when(zb == k)
            def _():
                attend(k)

        @pl.when(i < 4)
        def _():
            att_copy(zb, zl).start()

        return carry

    lax.fori_loop(1, 5, block_step, 0)
    att_in[zl] = att_out[zl]
    pick = (align_ref[...] - c * BLK == lax.broadcasted_iota(jnp.int32, (BLK, BLK), 0)).astype(BF16).T

    @pl.when(at_edge)
    def _():
        for t in (1, 2):
            wq_near(t, y * 2 + zh).wait_send()
            wo_near(t, y * 2 + zh).wait_send()

    loop(1, 16, lambda i: sc_copy(i, c).wait_send())
    for half_z in (0, 1):
        loop(1, 8, lambda i: wg_copy(i, y, half_z).wait_send())
        loop(1, 8, lambda i: wo_copy(i, y, half_z).wait_send())

    for n, s in enumerate(far_steps):
        wo2_copy(n, x_dev(s[0]), my_quarter).wait_send()
    for n in range(6):
        along_x(n, 0).wait_send()
    for n in range(4):
        over(n, slice_x(0, core)).wait_send()
    rc(wg.at[:, core], wg.at[:, core], wgx_s.at[0], wgx_r.at[0], (sib, c)).wait_send()

    ref = wo.at[:, :, 1 - core]
    rc(ref, ref, wo3_s.at[0], wo3_r.at[0], (sib, c)).wait_recv()
    for i in (1, 2, 3):
        slot = (zl - i + 4) % 4
        att_copy(slot, slot).wait_recv()

    attended = att_in[...].reshape(D, BLK).T
    total = jnp.zeros((BLK, 1), F32)
    for j in range(4):
        cols = pl.ds(j * 256, 256)
        branch = jnp.dot(attended, wo[j].reshape(D, 256), preferred_element_type=F32)
        hidden = (lat_scr[:, cols].astype(F32) + branch).astype(BF16)
        hid_ref[:, cols] = hidden
        diff = jnp.dot(pick, hidden, preferred_element_type=F32) - teach_ref[:, cols].astype(F32)
        total = total + jnp.sum(diff * diff, axis=1, keepdims=True)
    loss_ref[...] = jnp.broadcast_to(total * (1.0 / D), (BLK, 128)).T[0:1, :]

    rc(wo.at[:, :, core], wo.at[:, :, core], wo3_s.at[0], wo3_r.at[0], (sib, c)).wait_send()
    for i in (1, 2, 3):
        att_copy((zl + i) % 4, zl).wait_send()


def body(byte_ids, byte_table, w_conv, w_qkv, w_out, norm_gain, teacher, align):
    cos, sin = rope_tables(NCTX * BLK)
    vm = pl.BlockSpec(memory_space=pltpu.VMEM)
    dma = pltpu.SemaphoreType.DMA
    hidden, loss = pl.pallas_call(
        kernel,
        out_shape=(
            jax.ShapeDtypeStruct((BLK, D), BF16),
            jax.ShapeDtypeStruct((1, BLK), F32),
        ),
        in_specs=[vm] * 6 + [pl.BlockSpec(memory_space=pl.ANY)] * 3 + [vm],
        out_specs=(vm, vm),
        scratch_shapes=[
            pltpu.VMEM((3, 48, 128), BF16),
            pltpu.VMEM((3, 32, 384), BF16),
            pltpu.VMEM((NCTX, KW, BLK), jnp.int32),
            pltpu.VMEM((NCTX, 1, BLK), F32),
            pltpu.VMEM((8, 48, 128), BF16),
            pltpu.VMEM((2, 4, 4, 64, 512), BF16),
            pltpu.VMEM((16, 2, 32, 384), BF16),
            pltpu.VMEM((4, 16, 2, 32, 256), BF16),
            pltpu.VMEM((384, 1024), BF16),
            pltpu.VMEM((NCTX * BLK, HD), BF16),
            pltpu.VMEM((80, NCTX * BLK), BF16),
            pltpu.VMEM((4, HD, 4 * BLK), BF16),
            pltpu.VMEM((BLK, D), BF16),
            pltpu.VMEM((4, BLK, BLK), BF16),
            pltpu.VMEM((4, BLK, BLK), BF16),
            pltpu.VMEM((128, 128), F32),
            pltpu.VMEM((NCTX, D, BLK), BF16),
            pltpu.VMEM((NCTX, 128, BLK), F32),
            pltpu.VMEM((4, BLK, BLK), F32),
            pltpu.VMEM((D, BLK), F32),
            pltpu.VMEM((HD // 2, NCTX * BLK), F32),
            pltpu.VMEM((HD // 2, NCTX * BLK), F32),
            pltpu.VMEM((BLK, D), BF16),
            pltpu.SemaphoreType.DMA((3,)),
        ]
        + [
            dma((n,))
            for n in (16, 16, 16, 16, 12, 8, 4, 4, 3, 3, 6, 6, 4, 4, 18, 17, 1, 1, 18, 17, 4, 4, 1, 1, 4, 4)
        ],
        compiler_params=pltpu.CompilerParams(
            collective_id=0, has_side_effects=True, vmem_limit_bytes=56 * 2**20
        ),
    )(byte_ids, byte_table, w_conv, w_qkv, w_out, norm_gain.reshape(8, 128), jnp.asarray(cos), jnp.asarray(sin), teacher[0], align)
    return hidden[None], loss


def solution(mesh):
    in_specs = (
        P("fsdp", "ctx"),
        P(),
        P("fsdp", None),
        P("fsdp", None),
        P("fsdp", None),
        P(),
        P("fsdp", "ctx", None),
        P("fsdp", "ctx"),
    )
    out_specs = (P("fsdp", "ctx", None), P("fsdp", "ctx"))
    return jax.shard_map(body, mesh=mesh, in_specs=in_specs, out_specs=out_specs, check_vma=False)
```
